32 devices in a mesh: tm: 4 (over z), row: 2 (over x), col: 4 (over y, core).
Axes of the slice: x: 2, y: 2, z: 4, core: 2. Of those that a mesh axis runs over, the one named last changes fastest.
Arguments:
- occ_rows: float32 [1024, 512], P('row', ('tm', 'col')), may hold values from -1.2613447 to 1.2613447
- emp_rows: float32 [1024, 1536], P('row', ('tm', 'col')), may hold values from -0.9584147 to 0.9584147
- occ_cols: float32 [2048, 512], P('col', ('tm', 'row')), may hold values from -1.2613447 to 1.2613447
- emp_cols: float32 [2048, 1536], P('col', ('tm', 'row')), may hold values from -0.9584147 to 0.9584147
- occ_energy: float32 [1, 512], P(None, ('tm', 'col')), may hold values from 0.05 to 2
- emp_energy: float32 [1, 1536], P(None, ('tm', 'col')), may hold values from 0.05 to 2
- times: float32 [4], P('tm'), may hold values from 0.1 to 1.5
- freq_weight: float32 [4, 4], replicated, may hold values from -3 to 3
Outputs:
- spectrum: float32 [4, 2048, 1024], P('tm', 'col', 'row')
The draws below stay inside these ranges and needn't reach their ends.
All inputs are finite; a program needn't handle non-finite values.
Results may differ from the reference program's by a relative error of at most 0.00019.
Values sent between devices are 32-bit elements; how exact they have to be, the bound alone decides.
No kernel may reach another device: no remote copies, remote signals or barrier semaphores. Data moves between devices by JAX's collectives and lax.ppermute only.
A program may use at most 64 MiB of HBM per device.

```python
import math
import jax
import jax.numpy as jnp
from jax import lax

NOCC = 512
NEMP = 1536
GP = 2048
NTIME = 4
NFREQ = 4
R = 1024
CP = 2048


def levels(stream_key, extent, shards, low, top_value):
    loudness, own = 1.0, jax.random.fold_in(stream_key, 6)
    for axis_at, blocks in shards:
        draws = jnp.exp(jax.random.uniform(jax.random.fold_in(own, axis_at), (blocks,), jnp.float32, low / len(shards), top_value / len(shards)))
        loudness = loudness * jnp.repeat(draws, extent[axis_at] // blocks).reshape([-1 if axis == axis_at else 1 for axis in range(len(extent))])
    return loudness


def centred(rng, shape, width, limit, split=(), kind=jnp.bfloat16):
    entries = jax.random.normal(rng, shape, jnp.float32) * width
    if len(split) > 0:
        entries = levels(rng, shape, split, -0.22, 0.18) * entries
    return jnp.clip(entries, min=-limit, max=limit).astype(kind)


def setup_inputs(seed: int = 0) -> dict:
    key_list = jax.random.split(jax.random.key(seed), 9)
    occ_rows = centred(key_list[0], (R, NOCC), (NOCC ** -0.25), 1.2613447, ((0, 2), (1, 16)), jnp.float32)
    emp_rows = centred(key_list[1], (R, NEMP), (NEMP ** -0.25), 0.9584147, ((0, 2), (1, 16)), jnp.float32)
    occ_cols = centred(key_list[2], (CP, NOCC), (NOCC ** -0.25), 1.2613447, ((0, 4), (1, 8)), jnp.float32)
    emp_cols = centred(key_list[3], (CP, NEMP), (NEMP ** -0.25), 0.9584147, ((0, 4), (1, 8)), jnp.float32)
    occ_energy = jnp.clip(jnp.exp(math.log(2.0) - 3.6888794 * jax.random.uniform(key_list[4], (1, NOCC), jnp.float32) ** levels(key_list[4], (1, NOCC), ((1, 16),), -0.2, 0.2)), 0.05, 2.0)
    emp_energy = jnp.clip(jnp.exp(math.log(2.0) - 3.6888794 * jax.random.uniform(key_list[5], (1, NEMP), jnp.float32) ** levels(key_list[5], (1, NEMP), ((1, 16),), -0.2, 0.2)), 0.05, 2.0)
    times = jnp.clip(0.1 + 1.4 * jax.random.uniform(key_list[6], (NTIME,), jnp.float32) ** levels(key_list[6], (NTIME,), ((0, 4),), -0.2, 0.2), 0.1, 1.5)
    freq_weight = centred(key_list[7], (NFREQ, NTIME), 0.5, 3.0, (), jnp.float32)
    return {"occ_rows": occ_rows, "emp_rows": emp_rows, "occ_cols": occ_cols, "emp_cols": emp_cols, "occ_energy": occ_energy, "emp_energy": emp_energy, "times": times, "freq_weight": freq_weight}


def cosine_table(first_col, number_cols, first_mode, number_modes):
    column = first_col + jnp.arange(number_cols, dtype=jnp.int32)
    wave = first_mode + jnp.arange(number_modes, dtype=jnp.int32)
    phase = (2 * column[:, None] + 1) * wave[None, :] % (4 * GP)
    return jnp.sqrt(2.0 / GP) * jnp.cos(jnp.pi * phase.astype(jnp.float32) / (2.0 * GP))

def reference(occ_rows, emp_rows, occ_cols, emp_cols, occ_energy, emp_energy, times, freq_weight):
    precise = lax.Precision.HIGHEST
    table = cosine_table(0, occ_cols.shape[0], 0, GP)

    def one_time(instant):
        green_occ = jnp.dot(occ_rows * jnp.exp(-(instant * occ_energy)), occ_cols.T, precision=precise)
        green_emp = jnp.dot(emp_rows * jnp.exp(-(instant * emp_energy)), emp_cols.T, precision=precise)
        product = green_occ * green_emp
        return jnp.dot(table.T, product.T, precision=precise)
    modes = lax.map(one_time, times)
    return jnp.einsum('wt,tgr->wgr', freq_weight, modes, precision=precise)
```

```python
import functools

import jax
import jax.numpy as jnp
from jax import lax
from jax.experimental import pallas as pl
from jax.experimental.pallas import tpu as pltpu
from jax.sharding import PartitionSpec as P

GP = 2048
f32, bf16 = jnp.float32, jnp.bfloat16
VMEM_LIMIT = 32 * 1024 * 1024
EXTRA = 8
CHUNKS = 2
FINE = 32


def bits_of(size):
    return [1 << b for b in range(size.bit_length() - 1)][::-1]


def swap(value, axis, bit):
    size = lax.axis_size(axis)
    return lax.ppermute(value, axis, [(i, i ^ bit) for i in range(size)])


def unrelate(blocks, axis, dim):
    size, me = lax.axis_size(axis), lax.axis_index(axis)
    for bit in bits_of(size):
        shape = blocks.shape
        cut = blocks.reshape(*shape[:dim], -1, 2, bit, *shape[dim + 1 :])
        cut = jnp.where((me // bit) % 2 == 1, jnp.flip(cut, dim + 1), cut)
        blocks = cut.reshape(shape)
    return blocks


def pick(pieces, at):
    return lax.dynamic_index_in_dim(pieces, at, 0, False)


def exchange(pieces, axis, bits):
    me, low = lax.axis_index(axis), bits[-1] if bits else 1
    size, rest = pieces.shape[0], pieces.shape[1:]
    got = pieces[None]
    for bit in bits:
        got = got.reshape(got.shape[0], 2, -1, *rest)
        mine = (me // bit) % 2
        keep = lax.dynamic_index_in_dim(got, mine, 1, False)
        send = lax.dynamic_index_in_dim(got, 1 - mine, 1, False)
        got = jnp.stack([keep, swap(send, axis, bit)], 1)
        got = got.reshape(-1, *got.shape[2:])
    return got.reshape(size, *rest)


def split(value):
    high = value.astype(bf16)
    return high, (value - high.astype(f32)).astype(bf16)


def dot(a, b):
    return lax.dot_general(a, b, (((1,), (0,)), ((), ())), preferred_element_type=f32)


def green_kernel(chunk, slots, half, T, X, C, counts, *refs):
    occ_r, emp_r, occ_c, emp_c = counts
    place, weights, decay_occ, decay_emp = refs[:4]
    rows = refs[4 : 4 + 2 * T]
    cols = refs[4 + 2 * T : 6 + 2 * T]
    outs = refs[6 + 2 * T : 6 + 3 * T]
    flat, columns, s_high, s_low = refs[6 + 3 * T :]
    x, q = place[0], place[1]
    k_occ, k_emp = decay_occ.shape[1], decay_emp.shape[1]
    breadth = flat.shape[1]
    piece = cols[0].shape[-1]
    for s in range(T):
        for core in range(2):
            for d in range(C // 2):
                at = s * C + (q ^ (2 * d + core))
                block = rows[2 * s + core]
                flat[pl.ds(pl.multiple_of(at * occ_r, 8), occ_r), :] = block[d, chunk, 0:occ_r, :]
                flat[pl.ds(pl.multiple_of(k_occ + at * emp_r, 8), emp_r), :] = block[d, chunk, occ_r : occ_r + emp_r, :]
    for part in range(2):
        for i, (dx, dq) in enumerate(slots[part]):
            lanes = slice((dq // 2) * piece, (dq // 2) * piece + piece)
            for h in range(half):
                at = (part * half + h) * X + (x ^ dx)
                columns[pl.ds(pl.multiple_of(at * occ_c, 8), occ_c), lanes] = cols[part][i, h, 0:occ_c, :]
                columns[pl.ds(pl.multiple_of(k_occ + at * emp_c, 8), emp_c), lanes] = cols[part][i, h, occ_c : occ_c + emp_c, :]
    step = 128
    for kb in range((k_occ + k_emp) // step):
        at = kb * step
        turned = flat[at : at + step, :].T
        decay = decay_occ if at < k_occ else decay_emp
        first = at if at < k_occ else at - k_occ
        for t in range(T):
            high, low = split(turned * decay[t : t + 1, first : first + step])
            s_high[t * breadth : (t + 1) * breadth, at : at + step] = high
            s_low[t * breadth : (t + 1) * breadth, at : at + step] = low

    def green(lo, hi):
        c_high, c_low = split(columns[lo:hi, :])
        a_high, a_low = s_high[:, lo:hi], s_low[:, lo:hi]
        return dot(a_high, c_high) + dot(a_high, c_low) + dot(a_low, c_high)

    product = green(0, k_occ) * green(k_occ, k_occ + k_emp)
    for w in range(T):
        total = weights[w * T] * product[0:breadth, :]
        for t in range(1, T):
            total += weights[w * T + t] * product[t * breadth : (t + 1) * breadth, :]
        outs[w][...] = total


def table_kernel(near, far, high, low):
    share = far.shape[1]
    for h in range(share):
        c, s = far[0, h : h + 1, :], far[1, h : h + 1, :]
        for odd in range(2):
            value = c * near[2 * odd] - s * near[2 * odd + 1]
            a, b = split(value)
            high[odd, h * FINE : (h + 1) * FINE, :] = a
            low[odd, h * FINE : (h + 1) * FINE, :] = b


def mode_kernel(T, high, low, *refs):
    series = refs[: 2 * T]
    outs = refs[2 * T : -2]
    both, single = refs[-2:]
    breadth, width = series[0].shape
    step = width // 2 if width >= 256 else width
    groups = width // step
    at = 0
    for s in range(T):
        for d in range(groups):
            mine = series[2 * s][:, d * step : (d + 1) * step]
            e = groups - 1 - d
            theirs = series[2 * (s ^ (T - 1)) + 1][:, e * step : (e + 1) * step]
            for odd, value in enumerate((mine + theirs, mine - theirs)):
                a, b = split(value.T)
                both[odd, at : at + step, 0:breadth] = a
                both[odd, at : at + step, breadth:] = b
            at += step
    share = outs[0].shape[0] // 2
    for block, out in enumerate(outs):
        lines = slice(block * share, (block + 1) * share)
        for odd in range(2):
            twice = dot(high[odd, lines, :], both[odd])
            once = dot(low[odd, lines, :], both[odd, :, 0:breadth])
            out[pl.ds(odd, share, stride=2), :] = twice[:, :breadth] + twice[:, breadth:] + once


def place_kernel(place, *refs):
    pieces, out = refs[:-1], refs[-1]
    for i, piece in enumerate(pieces):
        breadth = piece.shape[2]
        for d in range(piece.shape[0]):
            at = ((place[1] // 2) ^ d) * CHUNKS + i
            out[0, :, pl.ds(pl.multiple_of(at * breadth, breadth), breadth)] = piece[d]


def per_device(occ_rows, emp_rows, occ_cols, emp_cols, occ_energy, emp_energy, times, freq_weight):
    T, X, C = lax.axis_size("tm"), lax.axis_size("row"), lax.axis_size("col")
    k, x, q = lax.axis_index("tm"), lax.axis_index("row"), lax.axis_index("col")
    number_rows, number_cols = occ_rows.shape[0], occ_cols.shape[0]
    occ_r, emp_r, occ_c, emp_c = (a.shape[1] for a in (occ_rows, emp_rows, occ_cols, emp_cols))
    n, m = occ_r + emp_r, occ_c + emp_c
    H = C // 2
    rp, jp = number_rows // (H * CHUNKS), number_cols // T
    half = T // 2
    k_occ, k_emp = occ_r * T * C, emp_r * T * C
    high_bits = [("col", b) for b in bits_of(C) if b > 1]
    row_bits = [("row", b) for b in bits_of(X)]

    turn = q >= C // 2
    col_t = jnp.concatenate([occ_cols, emp_cols], 1)
    col_t = jnp.where(turn, jnp.flip(col_t, 0), col_t).T.reshape(m, T, jp).transpose(1, 0, 2)
    mirror = jnp.where(turn, T - 1, 0)
    col_slots = [pick(col_t, k ^ mirror)] + [None] * (T - 1)
    for s in range(1, T):
        col_slots[s] = swap(pick(col_t, k ^ s ^ mirror), "tm", s)

    row_t = jnp.concatenate([occ_rows.T, emp_rows.T], 0).reshape(n, H, CHUNKS, rp).transpose(1, 2, 0, 3)
    energy = jnp.concatenate([occ_energy, emp_energy], 1)
    extra = jnp.zeros((EXTRA, rp), f32).at[0:1, :n].set(energy).at[1, :].set(times[0])
    row_t = jnp.concatenate([row_t, jnp.broadcast_to(extra, (H, CHUNKS, EXTRA, rp))], 2)
    own_rows = exchange(row_t, "col", [b for _, b in high_bits])
    row_slots = []
    for s in range(T):
        got = own_rows if s == 0 else swap(own_rows, "tm", s)
        row_slots += [got, swap(got, "col", 1)]

    cols, slots = [], []
    for first, order in ((0, row_bits + high_bits), (half, high_bits + row_bits)):
        value = jnp.stack(col_slots[first : first + half])[None]
        where = [(0, 0)]
        for axis, bit in order:
            value = jnp.concatenate([value, swap(value, axis, bit)], 0)
            where = where + [(dx ^ bit, dq) if axis == "row" else (dx, dq ^ bit) for dx, dq in where]
        cols.append(value)
        slots.append(where)

    heads = jnp.stack([r[:, 0, n : n + 2, :] for r in row_slots]).reshape(T, 2, H, 2, rp)
    levels = heads[:, :, :, 0, :n].transpose(0, 2, 1, 3).reshape(T, C, n)
    levels = unrelate(levels, "col", 1)
    instants = heads[:, 0, 0, 1, 0]

    def decays(energies):
        return jnp.exp(-(instants[:, None] * energies.reshape(1, -1)))

    decay_occ, decay_emp = decays(levels[:, :, :occ_r]), decays(levels[:, :, occ_r:])
    step = jnp.arange(T)
    weights = freq_weight[k ^ step][:, k ^ step].reshape(-1)
    place = jnp.stack([x, q]).astype(jnp.int32)

    smem = pl.BlockSpec(memory_space=pltpu.SMEM)
    vmem = pl.BlockSpec(memory_space=pltpu.VMEM)
    params = pltpu.CompilerParams(vmem_limit_bytes=VMEM_LIMIT)
    wide = H * jp
    own = []
    for chunk in range(CHUNKS):
        series = pl.pallas_call(
            functools.partial(green_kernel, chunk, slots, half, T, X, C, (occ_r, emp_r, occ_c, emp_c)),
            out_shape=[jax.ShapeDtypeStruct((rp, wide), f32)] * T,
            in_specs=[smem, smem] + [pl.BlockSpec()] * (2 + 2 * T + 2),
            scratch_shapes=[
                pltpu.VMEM((k_occ + k_emp, rp), f32),
                pltpu.VMEM((k_occ + k_emp, wide), f32),
                pltpu.VMEM((T * rp, k_occ + k_emp), bf16),
                pltpu.VMEM((T * rp, k_occ + k_emp), bf16),
            ],
            compiler_params=params,
            name="greens",
        )(place, weights, decay_occ, decay_emp, *row_slots, *cols)
        here = [series[0]] + [None] * (T - 1)
        for s in range(1, T):
            here[s] = swap(series[s], "tm", s)
        own.append(here)

    slot = jnp.arange(T, dtype=jnp.int32)[:, None, None]
    dq = 2 * jnp.arange(H, dtype=jnp.int32)[None, :, None]
    inner = jnp.arange(jp, dtype=jnp.int32)[None, None, :]
    source = q ^ dq
    lane = jnp.where(source >= C // 2, (T - 1 - (k ^ slot)) * 0 + (jp - 1 - inner), inner)
    column = (source * number_cols + (k ^ slot) * jp + lane).reshape(-1)
    odd_column = 2 * column + 1
    share = GP // C

    def angle(wave):
        phase = (odd_column[None, :] * wave[:, None]) % (4 * GP)
        return jnp.pi * phase.astype(f32) / (2.0 * GP)

    scale = jnp.sqrt(2.0 / GP)
    fine = 2 * jnp.arange(FINE, dtype=jnp.int32)
    per_block = share // (2 * FINE)
    blocks = q ^ (2 * jnp.arange(H, dtype=jnp.int32)[::-1])
    coarse = (blocks[:, None] * share + 2 * FINE * jnp.arange(per_block, dtype=jnp.int32)[None, :]).reshape(-1)
    even, odd, far = angle(fine), angle(fine + 1), angle(coarse)
    near = jnp.stack([scale * jnp.cos(even), scale * jnp.sin(even), scale * jnp.cos(odd), scale * jnp.sin(odd)])
    far = jnp.stack([jnp.cos(far), jnp.sin(far)])
    all_cols = T * wide
    t_high, t_low = pl.pallas_call(
        table_kernel,
        out_shape=[jax.ShapeDtypeStruct((2, H * share // 2, all_cols), bf16)] * 2,
        in_specs=[pl.BlockSpec()] * 2,
        out_specs=[vmem] * 2,
        compiler_params=params,
        name="cosines",
    )(near, far)

    pieces = []
    for chunk in range(CHUNKS):
        both = []
        for s in range(T):
            both += [own[chunk][s], swap(own[chunk][s], "col", 1)]
        made = pl.pallas_call(
            functools.partial(mode_kernel, T),
            out_shape=[jax.ShapeDtypeStruct((share, rp), f32)] * H,
            in_specs=[vmem] * 2 + [pl.BlockSpec()] * (2 * T),
            scratch_shapes=[pltpu.VMEM((2, all_cols, 2 * rp), bf16), pltpu.VMEM((8, 128), f32)],
            compiler_params=params,
            name="modes",
        )(t_high, t_low, *both)
        got = [made[H - 1]]
        for d in range(1, H):
            got.append(swap(made[H - 1 - d], "col", 2 * d))
        pieces.append(jnp.stack(got))
    return pl.pallas_call(
        place_kernel,
        out_shape=jax.ShapeDtypeStruct((1, share, number_rows), f32),
        in_specs=[smem] + [pl.BlockSpec()] * CHUNKS,
        compiler_params=params,
        name="assemble",
    )(place, *pieces)


def solution(mesh):
    return jax.shard_map(
        per_device,
        mesh=mesh,
        in_specs=(
            P("row", ("tm", "col")),
            P("row", ("tm", "col")),
            P("col", ("tm", "row")),
            P("col", ("tm", "row")),
            P(None, ("tm", "col")),
            P(None, ("tm", "col")),
            P("tm"),
            P(),
        ),
        out_specs=P("tm", "col", "row"),
        check_vma=False,
    )
```

```python
import functools

import jax
import jax.numpy as jnp
from jax import lax
from jax.experimental import pallas as pl
from jax.experimental.pallas import tpu as pltpu
from jax.sharding import PartitionSpec as P

GP = 2048
f32, bf16 = jnp.float32, jnp.bfloat16
VMEM_LIMIT = 32 * 1024 * 1024
EXTRA = 8
CHUNKS = 2
FINE = 32
HALVES_COST, SCALE_COST, GREENS_COST, TOKEN_COST, BEHIND = (12, 3), 1, 3, 3.6, 0


def bits_of(size):
    return [1 << b for b in range(size.bit_length() - 1)][::-1]


def swap(value, axis, bit):
    size = lax.axis_size(axis)
    return lax.ppermute(value, axis, [(i, i ^ bit) for i in range(size)])


def split(value):
    high = value.astype(bf16)
    return high, (value - high.astype(f32)).astype(bf16)


def dot(a, b):
    return lax.dot_general(a, b, (((1,), (0,)), ((), ())), preferred_element_type=f32)


def column_kernel(T, place, occ, emp, *outs):
    piece = outs[0].shape[1]
    for s in range(T):
        lines = pl.ds(pl.multiple_of((place[0] ^ s) * piece, piece), piece)
        outs[s][...] = jnp.concatenate([occ[lines, :].T, emp[lines, :].T], 0)


def row_kernel(place, times, occ, emp, occ_energy, emp_energy, _, *outs):
    chunks, lines, breadth = outs[0].shape
    occ_n, n = occ.shape[1], lines - EXTRA
    for d in range(len(outs)):
        for c in range(chunks):
            first = (((place[2] // 2) ^ d) * chunks + c) * breadth
            at = pl.ds(pl.multiple_of(first, breadth), breadth)
            outs[d][c, 0:occ_n, :] = occ[at, :].T
            outs[d][c, occ_n:n, :] = emp[at, :].T
            outs[d][c, n:, :] = jnp.full((EXTRA, breadth), times[0], f32)
            outs[d][c, n : n + 1, 0:occ_n] = occ_energy[...]
            outs[d][c, n : n + 1, occ_n:n] = emp_energy[...]


def scale_kernel(chunk, T, C, counts, *refs):
    occ_r, emp_r = counts
    n = occ_r + emp_r
    k_occ = occ_r * T * C
    place, rows = refs[0], refs[1:5]
    s_high, s_low, flat, falls = refs[5:]
    q = place[2]
    breadth, half = flat.shape[1], T // 2
    lane = lax.broadcasted_iota(jnp.int32, (1, breadth), 1)
    instants = jnp.zeros((1, breadth), f32)
    for s in range(T):
        instants = jnp.where(lane == s, rows[2 * (s // half)][s % half, 0, 0, n + 1 : n + 2, :], instants)
    for s in range(T):
        for core in range(2):
            for d in range(C // 2):
                at = s * C + (q ^ (2 * d + core))
                block = rows[2 * (s // half) + core].at[s % half, d]
                occ_at = pl.ds(pl.multiple_of(at * occ_r, 8), occ_r)
                emp_at = pl.ds(pl.multiple_of(k_occ + at * emp_r, 8), emp_r)
                flat[occ_at, :] = block[chunk, 0:occ_r, :]
                flat[emp_at, :] = block[chunk, occ_r:n, :]
                levels = block[0, n : n + EXTRA, :].T[0:n, 0:1]
                decay = jnp.exp(-(levels * instants))
                falls[occ_at, :] = decay[0:occ_r]
                falls[emp_at, :] = decay[occ_r:n]
    step = 128
    for at in range(0, flat.shape[0], step):
        turned = flat[at : at + step, :].T
        decay = falls[at : at + step, :].T
        for t in range(T):
            high, low = split(turned * decay[t : t + 1, :])
            s_high[t * breadth : (t + 1) * breadth, at : at + step] = high
            s_low[t * breadth : (t + 1) * breadth, at : at + step] = low


def halves_kernel(slots, C, X, counts, waits, *refs):
    occ_c, emp_c = counts
    place, cols = refs[0], refs[1 : 1 + len(slots)]
    high, low, columns = refs[1 + len(slots) + waits :]
    x, q, piece = place[1], place[2], cols[0].shape[-1]
    size = columns.shape[0] // (X * (occ_c + emp_c))
    k_occ = occ_c * X * size
    for part, where in enumerate(slots):
        for i, (dx, dq, s) in enumerate(where):
            lanes = slice((dq // 2) * piece, (dq // 2) * piece + piece)
            at = s * X + (x ^ dx)
            columns[pl.ds(pl.multiple_of(at * occ_c, 8), occ_c), lanes] = cols[part][i, 0:occ_c, :]
            columns[pl.ds(pl.multiple_of(k_occ + at * emp_c, 8), emp_c), lanes] = cols[part][i, occ_c : occ_c + emp_c, :]
    line = lax.broadcasted_iota(jnp.int32, (piece, piece), 0)
    lane = lax.broadcasted_iota(jnp.int32, (piece, piece), 1)
    for d in range(C // 2):
        lanes = slice(d * piece, (d + 1) * piece)
        goal = jnp.where((q ^ (2 * d)) >= C // 2, piece - 1 - lane, lane)
        turn = jnp.where(line == goal, 1.0, 0.0).astype(bf16)
        a, b = split(columns[:, lanes])
        high[:, lanes] = dot(a, turn).astype(bf16)
        low[:, lanes] = dot(b, turn).astype(bf16)


def green_kernel(T, k_occ, *refs):
    place, weights, s_high, s_low = refs[:4]
    halves, outs = refs[4:-T], refs[-T:]
    k, breadth = place[0], outs[0].shape[0]
    groups = len(halves) // 2

    def green(first, size):
        total = None
        for g in range(groups):
            share = size // groups
            lines = slice(first // groups, first // groups + share)
            lanes = slice(first + g * share, first + (g + 1) * share)
            c_high, c_low = halves[2 * g][lines, :], halves[2 * g + 1][lines, :]
            a_high, a_low = s_high[:, lanes], s_low[:, lanes]
            term = dot(a_high, c_high) + dot(a_high, c_low) + dot(a_low, c_high)
            total = term if total is None else total + term
        return total

    product = green(0, k_occ) * green(k_occ, s_high.shape[1] - k_occ)
    for w in range(T):
        total = weights[k ^ w, k] * product[0:breadth, :]
        for t in range(1, T):
            total += weights[k ^ w, k ^ t] * product[t * breadth : (t + 1) * breadth, :]
        outs[w][...] = total


def token_kernel(_, out):
    out[...] = jnp.zeros_like(out)


def pack_kernel(T, *refs):
    for s in range(T):
        refs[-1][s] = refs[s][...]


def cost(us):
    return pl.CostEstimate(flops=int(us * 1e9), bytes_accessed=0, transcendentals=0)


def table_kernel(near, far, high, low):
    share = far.shape[1]
    for h in range(share):
        c, s = far[0, h : h + 1, :], far[1, h : h + 1, :]
        for odd in range(2):
            value = c * near[2 * odd] - s * near[2 * odd + 1]
            a, b = split(value)
            high[odd, h * FINE : (h + 1) * FINE, :] = a
            low[odd, h * FINE : (h + 1) * FINE, :] = b


def mode_kernel(T, waits, high, low, *refs):
    here, there = refs[:2]
    outs, both = refs[2 + waits : -1], refs[-1]
    _, breadth, width = here.shape
    step = width // 2 if width >= 256 else width
    groups = width // step
    at = 0
    for s in range(T):
        for d in range(groups):
            mine = here[s, :, d * step : (d + 1) * step]
            e = groups - 1 - d
            theirs = there[s ^ (T - 1), :, e * step : (e + 1) * step]
            for odd, value in enumerate((mine + theirs, mine - theirs)):
                a, b = split(value.T)
                both[odd, at : at + step, 0:breadth] = a
                both[odd, at : at + step, breadth:] = b
            at += step
    share = outs[0].shape[0] // 2
    for block, out in enumerate(outs):
        lines = slice(block * share, (block + 1) * share)
        for odd in range(2):
            twice = dot(high[odd, lines, :], both[odd])
            once = dot(low[odd, lines, :], both[odd, :, 0:breadth])
            out[pl.ds(odd, share, stride=2), :] = twice[:, :breadth] + twice[:, breadth:] + once


def place_kernel(first, place, *refs):
    pieces, out, done = refs[:-2], refs[-2], refs[-1]
    copies = []
    for i, (chunk, d) in enumerate(first):
        breadth = pieces[i].shape[1]
        at = ((place[2] // 2) ^ d) * CHUNKS + chunk
        copies.append(pltpu.make_async_copy(pieces[i], out.at[0, :, pl.ds(pl.multiple_of(at * breadth, breadth), breadth)], done.at[i]))
    for copy in copies:
        copy.start()
    for copy in copies:
        copy.wait()


def per_device(occ_rows, emp_rows, occ_cols, emp_cols, occ_energy, emp_energy, times, freq_weight):
    T, X, C = lax.axis_size("tm"), lax.axis_size("row"), lax.axis_size("col")
    k, x, q = lax.axis_index("tm"), lax.axis_index("row"), lax.axis_index("col")
    number_rows, number_cols = occ_rows.shape[0], occ_cols.shape[0]
    occ_r, emp_r, occ_c, emp_c = (a.shape[1] for a in (occ_rows, emp_rows, occ_cols, emp_cols))
    n, m = occ_r + emp_r, occ_c + emp_c
    H = C // 2
    rp, jp = number_rows // (H * CHUNKS), number_cols // T
    k_occ, k_emp = occ_r * T * C, emp_r * T * C
    high_bits = [("col", b) for b in bits_of(C) if b > 1]
    row_bits = [("row", b) for b in bits_of(X)]

    place = jnp.stack([k, x, q]).astype(jnp.int32)
    smem = pl.BlockSpec(memory_space=pltpu.SMEM)
    vmem = pl.BlockSpec(memory_space=pltpu.VMEM)
    hbm = pl.BlockSpec(memory_space=pl.ANY)
    params = pltpu.CompilerParams(vmem_limit_bytes=VMEM_LIMIT)

    pieces = pl.pallas_call(
        functools.partial(column_kernel, T),
        out_shape=[jax.ShapeDtypeStruct((m, jp), f32)] * T,
        in_specs=[smem] + [pl.BlockSpec()] * 2,
        out_specs=[vmem] * T,
        compiler_params=params,
        cost_estimate=cost(0),
        name="columns",
    )(place, occ_cols, emp_cols)
    col_slots = [pieces[0]] + [swap(pieces[s], "tm", s) for s in range(1, T)]

    row_pieces = pl.pallas_call(
        row_kernel,
        out_shape=[jax.ShapeDtypeStruct((CHUNKS, n + EXTRA, rp), f32)] * H,
        in_specs=[smem, smem] + [pl.BlockSpec()] * 4 + [hbm],
        out_specs=[vmem] * H,
        compiler_params=params,
        cost_estimate=cost(0),
        name="rows",
    )(place, times, occ_rows, emp_rows, occ_energy, emp_energy, pieces[0])
    own_rows = jnp.stack([row_pieces[0]] + [swap(row_pieces[d], "col", 2 * d) for d in range(1, H)])
    got_rows = {0: own_rows}
    for bit in bits_of(T):
        for s in list(got_rows):
            got_rows[s ^ bit] = swap(got_rows[s], "tm", bit)
    row_slots = []
    for first in range(0, T, T // 2):
        mine = jnp.stack([got_rows[s] for s in range(first, first + T // 2)])
        row_slots += [mine, swap(mine, "col", 1)]

    groups = [list(range(T))[: T // 2], list(range(T))[T // 2 :]]
    cuts = [[groups[0]], [groups[1][: T // 4], groups[1][T // 4 :]]]
    orders = [[row_bits + high_bits], [row_bits + high_bits, high_bits + row_bits]]
    cols, slots = [], []
    for group, parts, ways in zip(groups, cuts, orders):
        there, where = [], []
        for part, order in zip(parts, ways):
            values = [(jnp.stack([col_slots[s] for s in part]), [(0, 0, group.index(s)) for s in part])]
            for axis, bit in order:
                if len(values) > 1:
                    values = [(jnp.concatenate([v for v, _ in values], 0), sum((w for _, w in values), []))]
                value, at = values[0]
                far = [(dx ^ bit, dq, f) if axis == "row" else (dx, dq ^ bit, f) for dx, dq, f in at]
                values.append((swap(value, axis, bit), far))
            there += [v for v, _ in values]
            where += [w for _, w in values]
        cols.append(there)
        slots.append(where)

    wide = H * jp

    slot = jnp.arange(T, dtype=jnp.int32)[:, None, None]
    dq = 2 * jnp.arange(H, dtype=jnp.int32)[None, :, None]
    inner = jnp.arange(jp, dtype=jnp.int32)[None, None, :]
    source = q ^ dq
    lane = jnp.where(source >= C // 2, jp - 1 - inner, inner)
    column = (source * number_cols + (k ^ slot) * jp + lane).reshape(-1)
    odd_column = 2 * column + 1
    share = GP // C

    def angle(wave):
        phase = (odd_column[None, :] * wave[:, None]) % (4 * GP)
        return jnp.pi * phase.astype(f32) / (2.0 * GP)

    scale = jnp.sqrt(2.0 / GP)
    fine = 2 * jnp.arange(FINE, dtype=jnp.int32)
    per_block = share // (2 * FINE)
    blocks = q ^ (2 * jnp.arange(H, dtype=jnp.int32)[::-1])
    coarse = (blocks[:, None] * share + 2 * FINE * jnp.arange(per_block, dtype=jnp.int32)[None, :]).reshape(-1)
    even, odd, far = angle(fine), angle(fine + 1), angle(coarse)
    near = jnp.stack([scale * jnp.cos(even), scale * jnp.sin(even), scale * jnp.cos(odd), scale * jnp.sin(odd)])
    far = jnp.stack([jnp.cos(far), jnp.sin(far)])
    all_cols = T * wide
    t_high, t_low = pl.pallas_call(
        table_kernel,
        out_shape=[jax.ShapeDtypeStruct((2, H * share // 2, all_cols), bf16)] * 2,
        in_specs=[pl.BlockSpec()] * 2,
        out_specs=[vmem] * 2,
        compiler_params=params,
        cost_estimate=cost(0),
        name="cosines",
    )(near, far)

    halves, waits = [], [t_high, row_slots[1]]
    for g, group in enumerate(groups):
        got = pl.pallas_call(
            functools.partial(halves_kernel, slots[g], C, X, (occ_c, emp_c), len(waits)),
            out_shape=[jax.ShapeDtypeStruct(((k_occ + k_emp) // len(groups), wide), bf16)] * 2,
            in_specs=[smem] + [pl.BlockSpec()] * len(cols[g]) + [hbm] * len(waits),
            out_specs=[vmem] * 2,
            scratch_shapes=[pltpu.VMEM(((k_occ + k_emp) // len(groups), wide), f32)],
            compiler_params=params,
            cost_estimate=cost(HALVES_COST[g]),
            name="halves",
        )(place, *cols[g], *waits)
        halves += got
        waits = [got[0]]

    own = []
    for chunk in range(CHUNKS):
        scaled = pl.pallas_call(
            functools.partial(scale_kernel, chunk, T, C, (occ_r, emp_r)),
            out_shape=[jax.ShapeDtypeStruct((T * rp, k_occ + k_emp), bf16)] * 2,
            in_specs=[smem] + [pl.BlockSpec()] * len(row_slots),
            out_specs=[vmem] * 2,
            scratch_shapes=[pltpu.VMEM((k_occ + k_emp, rp), f32)] * 2,
            compiler_params=params,
            cost_estimate=cost(SCALE_COST),
            name="scale",
        )(place, *row_slots)
        series = pl.pallas_call(
            functools.partial(green_kernel, T, k_occ),
            out_shape=[jax.ShapeDtypeStruct((rp, wide), f32)] * T,
            in_specs=[smem, smem] + [vmem] * (2 + len(halves)),
            out_specs=[vmem] * T,
            compiler_params=params,
            cost_estimate=cost(GREENS_COST),
            name="greens",
        )(place, freq_weight, *scaled, *halves)
        here = [series[0]] + [None] * (T - 1)
        for s in range(T - 1, 0, -1):
            here[s] = swap(series[s], "tm", s)
        own.append(here)

    def assemble(parts, before):
        return pl.pallas_call(
            functools.partial(place_kernel, [at for at, _ in parts]),
            out_shape=jax.ShapeDtypeStruct((1, share, number_rows), f32),
            in_specs=[smem] + [hbm] * (len(parts) + len(before)),
            out_specs=hbm,
            scratch_shapes=[pltpu.SemaphoreType.DMA((len(parts),))],
            input_output_aliases={1 + len(parts): 0} if before else {},
            compiler_params=params,
            cost_estimate=cost(0),
            name="assemble",
        )(place, *[part for _, part in parts], *before)

    early, late = [], []
    for chunk in range(CHUNKS):
        behind = [own[chunk + 1][BEHIND]] if chunk + 1 < CHUNKS else []
        mine = pl.pallas_call(
            functools.partial(pack_kernel, T),
            out_shape=jax.ShapeDtypeStruct((T, rp, wide), f32),
            in_specs=[vmem] * T + [hbm] * len(behind),
            out_specs=vmem,
            compiler_params=params,
            cost_estimate=cost(0),
            name="pack",
        )(*own[chunk], *behind)
        waits = [
            pl.pallas_call(
                token_kernel,
                out_shape=jax.ShapeDtypeStruct((8, 128), f32),
                in_specs=[hbm],
                compiler_params=params,
                cost_estimate=cost(TOKEN_COST),
                name="token",
            )(part)
            for _, part in late
        ]
        made = pl.pallas_call(
            functools.partial(mode_kernel, T, len(waits)),
            out_shape=[jax.ShapeDtypeStruct((share, rp), f32)] * H,
            in_specs=[vmem] * 4 + [hbm] * len(waits),
            out_specs=[vmem] * H,
            scratch_shapes=[pltpu.VMEM((2, all_cols, 2 * rp), bf16)],
            compiler_params=params,
            cost_estimate=cost(0),
            name="modes",
        )(t_high, t_low, mine, swap(mine, "col", 1), *waits)
        early = early + late + [((chunk, 0), made[H - 1])]
        late = [((chunk, d), swap(made[H - 1 - d], "col", 2 * d)) for d in range(1, H)]
    return assemble(late, [assemble(early, [])])


def solution(mesh):
    return jax.shard_map(
        per_device,
        mesh=mesh,
        in_specs=(
            P("row", ("tm", "col")),
            P("row", ("tm", "col")),
            P("col", ("tm", "row")),
            P("col", ("tm", "row")),
            P(None, ("tm", "col")),
            P(None, ("tm", "col")),
            P("tm"),
            P(),
        ),
        out_specs=P("tm", "col", "row"),
        check_vma=False,
    )
```

```python
import functools

import jax
import jax.numpy as jnp
from jax import lax
from jax.experimental import pallas as pl
from jax.experimental.pallas import tpu as pltpu
from jax.sharding import PartitionSpec as P

GP = 2048
f32, bf16 = jnp.float32, jnp.bfloat16
VMEM_LIMIT = 32 * 1024 * 1024
VMEM_ALL = 60 * 1024 * 1024
EXTRA = 8
CHUNKS = 2
FINE = 32
HALVES_COST, SCALE_COST, GREENS_COST, TOKEN_COST, BEHIND, GATE = (12, 8), (0, 0), 3, 3.6, 0, 1


def bits_of(size):
    return [1 << b for b in range(size.bit_length() - 1)][::-1]


def swap(value, axis, bit):
    size = lax.axis_size(axis)
    return lax.ppermute(value, axis, [(i, i ^ bit) for i in range(size)])


def split(value):
    high = value.astype(bf16)
    return high, (value - high.astype(f32)).astype(bf16)


def dot(a, b):
    return lax.dot_general(a, b, (((1,), (0,)), ((), ())), preferred_element_type=f32)


def prepare_kernel(T, H, times, *refs):
    sources, slices, blocks = refs[:6], refs[6 : 6 + T], refs[6 + T : 6 + T + H]
    here, done = refs[6 + T + H : -1], refs[-1]
    copies = [pltpu.make_async_copy(a, b, done.at[i]) for i, (a, b) in enumerate(zip(sources, here))]
    for copy in copies:
        copy.start()
    for copy in copies:
        copy.wait()
    occ_c, emp_c, occ_r, emp_r, occ_energy, emp_energy = here
    k, q = lax.axis_index("tm"), lax.axis_index("col")
    n, piece = occ_c.shape[0], slices[0].shape[1]
    for s in range(T):
        for one in range(T) if piece % 128 else (None,):
            @pl.when(True if one is None else (k ^ s) == one)
            def _():
                first = pl.multiple_of((k ^ s) * piece, piece) if one is None else one * piece
                slices[s][0:n, :] = occ_c[:, pl.ds(first, piece)]
                slices[s][n:-EXTRA, :] = emp_c[:, pl.ds(first, piece)]
        slices[s][-EXTRA:, :] = jnp.full((EXTRA, piece), times[0], f32)
    chunks, lines, breadth = blocks[0].shape
    occ_n, n = occ_r.shape[0], lines - EXTRA
    for d in range(H):
        for c in range(chunks):
            first = (((q // 2) ^ d) * chunks + c) * breadth
            at = pl.ds(pl.multiple_of(first, breadth), breadth)
            blocks[d][c, 0:occ_n, :] = occ_r[:, at]
            blocks[d][c, occ_n:n, :] = emp_r[:, at]
            blocks[d][c, n:, :] = jnp.zeros((EXTRA, breadth), f32)
            blocks[d][c, n : n + 1, 0:occ_n] = occ_energy[...]
            blocks[d][c, n : n + 1, occ_n:n] = emp_energy[...]


def gate_kernel(waits, *refs):
    pieces, out = refs[: -1 - waits], refs[-1]
    for s, piece in enumerate(pieces):
        out[s] = piece[0 : out.shape[1], :]


def scale_kernel(chunk, T, C, counts, *refs):
    occ_r, emp_r = counts
    n = occ_r + emp_r
    place, rows, (s_high, s_low, flat, falls) = refs[0], refs[1:3], refs[-4:]
    instant, slots = refs[3 : 3 + T], rows[0].shape[0]
    k_occ = occ_r * slots * C
    q = place[2]
    breadth = flat.shape[1]
    lane = lax.broadcasted_iota(jnp.int32, (1, breadth), 1)
    instants = jnp.zeros((1, breadth), f32)
    for t in range(T):
        instants = jnp.where(lane == t, instant[t][-1:, 0:1], instants)
    for s in range(slots):
        for core in range(2):
            for d in range(C // 2):
                at = s * C + (q ^ (2 * d + core))
                block = rows[core].at[s, d]
                occ_at = pl.ds(pl.multiple_of(at * occ_r, 8), occ_r)
                emp_at = pl.ds(pl.multiple_of(k_occ + at * emp_r, 8), emp_r)
                flat[occ_at, :] = block[chunk, 0:occ_r, :]
                flat[emp_at, :] = block[chunk, occ_r:n, :]
                levels = block[chunk, n : n + EXTRA, :].T[0:n, 0:1]
                decay = jnp.exp(-(levels * instants))
                falls[occ_at, :] = decay[0:occ_r]
                falls[emp_at, :] = decay[occ_r:n]
    step = 128
    for at in range(0, flat.shape[0], step):
        turned = flat[at : at + step, :].T
        decay = falls[at : at + step, :].T
        for t in range(T):
            high, low = split(turned * decay[t : t + 1, :])
            s_high[t * breadth : (t + 1) * breadth, at : at + step] = high
            s_low[t * breadth : (t + 1) * breadth, at : at + step] = low


def halves_kernel(slots, C, X, counts, waits, *refs):
    occ_c, emp_c = counts
    place, cols = refs[0], refs[1 : 1 + len(slots)]
    high, low, columns = refs[1 + len(slots) + waits :]
    x, q, piece = place[1], place[2], cols[0].shape[-1]
    size = columns.shape[0] // (X * (occ_c + emp_c))
    k_occ = occ_c * X * size
    for part, where in enumerate(slots):
        for i, (dx, dq, s) in enumerate(where):
            lanes = slice((dq // 2) * piece, (dq // 2) * piece + piece)
            at = s * X + (x ^ dx)
            columns[pl.ds(pl.multiple_of(at * occ_c, 8), occ_c), lanes] = cols[part][i, 0:occ_c, :]
            columns[pl.ds(pl.multiple_of(k_occ + at * emp_c, 8), emp_c), lanes] = cols[part][i, occ_c : occ_c + emp_c, :]
    line = lax.broadcasted_iota(jnp.int32, (piece, piece), 0)
    lane = lax.broadcasted_iota(jnp.int32, (piece, piece), 1)
    for d in range(C // 2):
        lanes = slice(d * piece, (d + 1) * piece)
        goal = jnp.where((q ^ (2 * d)) >= C // 2, piece - 1 - lane, lane)
        turn = jnp.where(line == goal, 1.0, 0.0).astype(bf16)
        a, b = split(columns[:, lanes])
        high[:, lanes] = dot(a, turn).astype(bf16)
        low[:, lanes] = dot(b, turn).astype(bf16)


def green_kernel(T, groups, k_occ, *refs):
    place, weights = refs[:2]
    scaled, halves, outs = refs[2 : 2 + 2 * groups], refs[2 + 2 * groups : -T], refs[-T:]
    k, breadth = place[0], outs[0].shape[0]

    def green(lines):
        total = None
        for g in range(groups):
            a_high, a_low = scaled[2 * g][:, lines], scaled[2 * g + 1][:, lines]
            c_high, c_low = halves[2 * g][lines, :], halves[2 * g + 1][lines, :]
            term = dot(a_high, c_high) + dot(a_high, c_low) + dot(a_low, c_high)
            total = term if total is None else total + term
        return total

    product = green(slice(0, k_occ)) * green(slice(k_occ, scaled[0].shape[1]))
    for w in range(T):
        total = weights[k ^ w, k] * product[0:breadth, :]
        for t in range(1, T):
            total += weights[k ^ w, k ^ t] * product[t * breadth : (t + 1) * breadth, :]
        outs[w][...] = total


def token_kernel(_, out):
    out[...] = jnp.zeros_like(out)


def pack_kernel(order, *refs):
    for i, s in enumerate(order):
        refs[-1][s] = refs[i][...]


def cost(us):
    return pl.CostEstimate(flops=int(us * 1e9), bytes_accessed=0, transcendentals=0)


def table_kernel(near, far, high, low):
    share = far.shape[1]
    for h in range(share):
        c, s = far[0, h : h + 1, :], far[1, h : h + 1, :]
        for odd in range(2):
            value = c * near[2 * odd] - s * near[2 * odd + 1]
            a, b = split(value)
            high[odd, h * FINE : (h + 1) * FINE, :] = a
            low[odd, h * FINE : (h + 1) * FINE, :] = b


def fold_kernel(block, waits, high, low, *refs):
    here, there = refs[:2]
    out, both = refs[2 + waits :]
    T, breadth, width = here.shape
    step = width // 2 if width >= 256 else width
    groups = width // step
    at = 0
    for s in range(T):
        for d in range(groups):
            mine = here[s, :, d * step : (d + 1) * step]
            e = groups - 1 - d
            theirs = there[s ^ (T - 1), :, e * step : (e + 1) * step]
            for odd, value in enumerate((mine + theirs, mine - theirs)):
                a, b = split(value.T)
                both[odd, at : at + step, 0:breadth] = a
                both[odd, at : at + step, breadth:] = b
            at += step
    mode_kernel(block, 0, high, low, both, out)


def mode_kernel(block, waits, high, low, both, *refs):
    out = refs[-1]
    share, breadth = out.shape[0] // 2, out.shape[1]
    lines = slice(block * share, (block + 1) * share)
    for odd in range(2):
        twice = dot(high[odd, lines, :], both[odd])
        once = dot(low[odd, lines, :], both[odd, :, 0:breadth])
        out[pl.ds(odd, share, stride=2), :] = twice[:, :breadth] + twice[:, breadth:] + once


def place_kernel(first, place, *refs):
    pieces, out, done = refs[:-2], refs[-2], refs[-1]
    copies = []
    for i, (chunk, d) in enumerate(first):
        breadth = pieces[i].shape[1]
        at = ((place[2] // 2) ^ d) * CHUNKS + chunk
        copies.append(pltpu.make_async_copy(pieces[i], out.at[0, :, pl.ds(pl.multiple_of(at * breadth, breadth), breadth)], done.at[i]))
    for copy in copies:
        copy.start()
    for copy in copies:
        copy.wait()


def per_device(occ_rows, emp_rows, occ_cols, emp_cols, occ_energy, emp_energy, times, freq_weight):
    T, X, C = lax.axis_size("tm"), lax.axis_size("row"), lax.axis_size("col")
    k, x, q = lax.axis_index("tm"), lax.axis_index("row"), lax.axis_index("col")
    number_rows, number_cols = occ_rows.shape[0], occ_cols.shape[0]
    occ_r, emp_r, occ_c, emp_c = (a.shape[1] for a in (occ_rows, emp_rows, occ_cols, emp_cols))
    n, m = occ_r + emp_r, occ_c + emp_c
    H = C // 2
    rp, jp = number_rows // (H * CHUNKS), number_cols // T
    k_occ, k_emp = occ_r * T * C, emp_r * T * C
    high_bits = [("col", b) for b in bits_of(C) if b > 1]
    row_bits = [("row", b) for b in bits_of(X)]

    place = jnp.stack([k, x, q]).astype(jnp.int32)
    smem = pl.BlockSpec(memory_space=pltpu.SMEM)
    vmem = pl.BlockSpec(memory_space=pltpu.VMEM)
    hbm = pl.BlockSpec(memory_space=pl.ANY)
    params = pltpu.CompilerParams(vmem_limit_bytes=VMEM_LIMIT)

    sources = [occ_cols.T, emp_cols.T, occ_rows.T, emp_rows.T, occ_energy, emp_energy]
    prepared = pl.pallas_call(
        functools.partial(prepare_kernel, T, H),
        out_shape=[jax.ShapeDtypeStruct((m + EXTRA, jp), f32)] * T + [jax.ShapeDtypeStruct((CHUNKS, n + EXTRA, rp), f32)] * H,
        in_specs=[smem] + [hbm] * len(sources),
        out_specs=[vmem] * (T + H),
        scratch_shapes=[pltpu.VMEM(a.shape, f32) for a in sources] + [pltpu.SemaphoreType.DMA((len(sources),))],
        compiler_params=pltpu.CompilerParams(vmem_limit_bytes=VMEM_ALL),
        cost_estimate=cost(0),
        name="prepare",
    )(times, *sources)
    pieces, row_pieces = prepared[:T], prepared[T:]
    col_slots = [pieces[0]] + [swap(pieces[s], "tm", s) for s in range(1, T)]
    own_rows = jnp.stack([row_pieces[0]] + [swap(row_pieces[d], "col", 2 * d) for d in range(1, H)])
    got_rows = {0: own_rows}
    for bit in bits_of(T):
        for s in list(got_rows):
            got_rows[s ^ bit] = swap(got_rows[s], "tm", bit)
    early_rows = jnp.stack([got_rows[s] for s in range(T // 2)])
    row_slots = [[early_rows, swap(early_rows, "col", 1)]]

    groups = [list(range(T))[: T // 2], list(range(T))[T // 2 :]]
    cuts = [[groups[0]], [groups[1][: T // 4], groups[1][T // 4 :]]]
    orders = [[row_bits + high_bits], [row_bits + high_bits, high_bits + row_bits]]
    cols, slots, firsts = [], [], []
    for group, parts, ways in zip(groups, cuts, orders):
        there, where = [], []
        for part, order in zip(parts, ways):
            waits = firsts[:1] if GATE and group is groups[1] else []
            value = pl.pallas_call(
                functools.partial(gate_kernel, len(waits)),
                out_shape=jax.ShapeDtypeStruct((len(part), m, jp), f32),
                in_specs=[vmem] * len(part) + [hbm] * len(waits),
                out_specs=vmem,
                compiler_params=params,
                cost_estimate=cost(0),
                name="gate",
            )(*[col_slots[s] for s in part], *waits)
            values = [(value, [(0, 0, group.index(s)) for s in part])]
            for axis, bit in order:
                if len(values) > 1:
                    values = [(jnp.concatenate([v for v, _ in values], 0), sum((w for _, w in values), []))]
                value, at = values[0]
                far = [(dx ^ bit, dq, f) if axis == "row" else (dx, dq ^ bit, f) for dx, dq, f in at]
                values.append((swap(value, axis, bit), far))
                firsts.append(values[-1][0])
            there += [v for v, _ in values]
            where += [w for _, w in values]
        cols.append(there)
        slots.append(where)

    wide = H * jp

    slot = jnp.arange(T, dtype=jnp.int32)[:, None, None]
    dq = 2 * jnp.arange(H, dtype=jnp.int32)[None, :, None]
    inner = jnp.arange(jp, dtype=jnp.int32)[None, None, :]
    source = q ^ dq
    lane = jnp.where(source >= C // 2, jp - 1 - inner, inner)
    column = (source * number_cols + (k ^ slot) * jp + lane).reshape(-1)
    odd_column = 2 * column + 1
    share = GP // C

    def angle(wave):
        phase = (odd_column[None, :] * wave[:, None]) % (4 * GP)
        return jnp.pi * phase.astype(f32) / (2.0 * GP)

    scale = jnp.sqrt(2.0 / GP)
    fine = 2 * jnp.arange(FINE, dtype=jnp.int32)
    per_block = share // (2 * FINE)
    blocks = q ^ (2 * jnp.arange(H, dtype=jnp.int32)[::-1])
    coarse = (blocks[:, None] * share + 2 * FINE * jnp.arange(per_block, dtype=jnp.int32)[None, :]).reshape(-1)
    even, odd, far = angle(fine), angle(fine + 1), angle(coarse)
    near = jnp.stack([scale * jnp.cos(even), scale * jnp.sin(even), scale * jnp.cos(odd), scale * jnp.sin(odd)])
    far = jnp.stack([jnp.cos(far), jnp.sin(far)])
    all_cols = T * wide
    t_high, t_low = pl.pallas_call(
        table_kernel,
        out_shape=[jax.ShapeDtypeStruct((2, H * share // 2, all_cols), bf16)] * 2,
        in_specs=[pl.BlockSpec()] * 2,
        out_specs=[vmem] * 2,
        compiler_params=params,
        cost_estimate=cost(0),
        name="cosines",
    )(near, far)

    halves, waits = [], [t_high]
    for g, group in enumerate(groups):
        got = pl.pallas_call(
            functools.partial(halves_kernel, slots[g], C, X, (occ_c, emp_c), len(waits)),
            out_shape=[jax.ShapeDtypeStruct(((k_occ + k_emp) // len(groups), wide), bf16)] * 2,
            in_specs=[smem] + [pl.BlockSpec()] * len(cols[g]) + [hbm] * len(waits),
            out_specs=[vmem] * 2,
            scratch_shapes=[pltpu.VMEM(((k_occ + k_emp) // len(groups), wide), f32)],
            compiler_params=params,
            cost_estimate=cost(HALVES_COST[g]),
            name="halves",
        )(place, *cols[g], *waits)
        halves += got
        waits = [got[0]]

    own, instants = [], [slot[-EXTRA:] for slot in col_slots]
    for chunk in range(CHUNKS):
        scaled = []
        for g in range(len(groups)):
            if len(row_slots) == g:
                late_rows = pl.pallas_call(
                    functools.partial(pack_kernel, range(T // 2)),
                    out_shape=jax.ShapeDtypeStruct(early_rows.shape, f32),
                    in_specs=[vmem] * (T // 2) + [hbm] * 2,
                    out_specs=vmem,
                    compiler_params=params,
                    cost_estimate=cost(0),
                    name="pack",
                )(*[got_rows[s] for s in groups[g]], scaled[0], halves[0])
                row_slots.append([late_rows, swap(late_rows, "col", 1)])
            k_group = (k_occ + k_emp) // len(groups)
            scaled += pl.pallas_call(
                functools.partial(scale_kernel, chunk, T, C, (occ_r, emp_r)),
                out_shape=[jax.ShapeDtypeStruct((T * rp, k_group), bf16)] * 2,
                in_specs=[smem] + [pl.BlockSpec()] * 2 + [vmem] * T + [hbm] * len(own),
                out_specs=[vmem] * 2,
                scratch_shapes=[pltpu.VMEM((k_group, rp), f32)] * 2,
                compiler_params=params,
                cost_estimate=cost(SCALE_COST[g]),
                name="scale",
            )(place, *row_slots[g], *instants, *[here[0] for here in own])
        series = pl.pallas_call(
            functools.partial(green_kernel, T, len(groups), k_occ // len(groups)),
            out_shape=[jax.ShapeDtypeStruct((rp, wide), f32)] * T,
            in_specs=[smem, smem] + [vmem] * (len(scaled) + len(halves)),
            out_specs=[vmem] * T,
            compiler_params=params,
            cost_estimate=cost(GREENS_COST),
            name="greens",
        )(place, freq_weight, *scaled, *halves)
        here = [series[0]] + [None] * (T - 1)
        for s in range(T - 1, 0, -1):
            here[s] = swap(series[s], "tm", s)
        own.append(here)

    def assemble(parts, before):
        return pl.pallas_call(
            functools.partial(place_kernel, [at for at, _ in parts]),
            out_shape=jax.ShapeDtypeStruct((1, share, number_rows), f32),
            in_specs=[smem] + [hbm] * (len(parts) + len(before)),
            out_specs=hbm,
            scratch_shapes=[pltpu.SemaphoreType.DMA((len(parts),))],
            input_output_aliases={1 + len(parts): 0} if before else {},
            compiler_params=params,
            cost_estimate=cost(0),
            name="assemble",
        )(place, *[part for _, part in parts], *before)

    early, late = [], []
    for chunk in range(CHUNKS):
        behind = [own[chunk + 1][BEHIND]] if chunk + 1 < CHUNKS else []
        mine = pl.pallas_call(
            functools.partial(pack_kernel, range(T)),
            out_shape=jax.ShapeDtypeStruct((T, rp, wide), f32),
            in_specs=[vmem] * T + [hbm] * len(behind),
            out_specs=vmem,
            compiler_params=params,
            cost_estimate=cost(0),
            name="pack",
        )(*own[chunk], *behind)
        waits = [
            pl.pallas_call(
                token_kernel,
                out_shape=jax.ShapeDtypeStruct((8, 128), f32),
                in_specs=[hbm],
                compiler_params=params,
                cost_estimate=cost(TOKEN_COST),
                name="token",
            )(part)
            for _, part in late
        ]
        shape = jax.ShapeDtypeStruct((share, rp), f32)
        made = pl.pallas_call(
            functools.partial(fold_kernel, 0, len(waits)),
            out_shape=[shape, jax.ShapeDtypeStruct((2, all_cols, 2 * rp), bf16)],
            in_specs=[vmem] * 4 + [hbm] * len(waits),
            out_specs=[vmem] * 2,
            compiler_params=params,
            cost_estimate=cost(0),
            name="modes",
        )(t_high, t_low, mine, swap(mine, "col", 1), *waits)
        made, both = [made[0]], made[1]
        for block in range(1, H):
            made.append(
                pl.pallas_call(
                    functools.partial(mode_kernel, block, 0),
                    out_shape=shape,
                    in_specs=[vmem] * 3,
                    out_specs=vmem,
                    compiler_params=params,
                    cost_estimate=cost(0),
                    name="modes",
                )(t_high, t_low, both)
            )
        early = early + late + [((chunk, 0), made[H - 1])]
        late = [((chunk, d), swap(made[H - 1 - d], "col", 2 * d)) for d in range(1, H)]
    return assemble(late, [assemble(early, [])])


def solution(mesh):
    return jax.shard_map(
        per_device,
        mesh=mesh,
        in_specs=(
            P("row", ("tm", "col")),
            P("row", ("tm", "col")),
            P("col", ("tm", "row")),
            P("col", ("tm", "row")),
            P(None, ("tm", "col")),
            P(None, ("tm", "col")),
            P("tm"),
            P(),
        ),
        out_specs=P("tm", "col", "row"),
        check_vma=False,
    )
```

```python
import functools

import jax
import jax.numpy as jnp
from jax import lax
from jax.experimental import pallas as pl
from jax.experimental.pallas import tpu as pltpu
from jax.sharding import PartitionSpec as P

GP = 2048
f32, bf16 = jnp.float32, jnp.bfloat16
VMEM_LIMIT = 32 * 1024 * 1024
VMEM_ALL = 60 * 1024 * 1024
EXTRA = 8
CHUNKS = 2
FINE = 32
HALVES_COST, SCALE_COST, GREENS_COST, TOKEN_COST, BEHIND, GATE = (12, 8), (0, 0), 3, 3.6, 0, 1


def bits_of(size):
    return [1 << b for b in range(size.bit_length() - 1)][::-1]


def swap(value, axis, bit):
    size = lax.axis_size(axis)
    return lax.ppermute(value, axis, [(i, i ^ bit) for i in range(size)])


def split(value):
    high = value.astype(bf16)
    return high, (value - high.astype(f32)).astype(bf16)


def dot(a, b):
    return lax.dot_general(a, b, (((1,), (0,)), ((), ())), preferred_element_type=f32)


def prepare_kernel(T, H, times, *refs):
    sources, slices, blocks = refs[:6], refs[6 : 6 + T], refs[6 + T : 6 + T + H]
    here, done = refs[6 + T + H : -1], refs[-1]
    copies = [pltpu.make_async_copy(a, b, done.at[i]) for i, (a, b) in enumerate(zip(sources, here))]
    for copy in copies:
        copy.start()
    for copy in copies:
        copy.wait()
    occ_c, emp_c, occ_r, emp_r, occ_energy, emp_energy = here
    k, q = lax.axis_index("tm"), lax.axis_index("col")
    n, piece = occ_c.shape[0], slices[0].shape[1]
    for s in range(T):
        for one in range(T) if piece % 128 else (None,):
            @pl.when(True if one is None else (k ^ s) == one)
            def _():
                first = pl.multiple_of((k ^ s) * piece, piece) if one is None else one * piece
                slices[s][0:n, :] = occ_c[:, pl.ds(first, piece)]
                slices[s][n:-EXTRA, :] = emp_c[:, pl.ds(first, piece)]
        slices[s][-EXTRA:, :] = jnp.full((EXTRA, piece), times[0], f32)
    chunks, lines, breadth = blocks[0].shape
    occ_n, n = occ_r.shape[0], lines - EXTRA
    for d in range(H):
        for c in range(chunks):
            first = (((q // 2) ^ d) * chunks + c) * breadth
            at = pl.ds(pl.multiple_of(first, breadth), breadth)
            blocks[d][c, 0:occ_n, :] = occ_r[:, at]
            blocks[d][c, occ_n:n, :] = emp_r[:, at]
            blocks[d][c, n:, :] = jnp.zeros((EXTRA, breadth), f32)
            blocks[d][c, n : n + 1, 0:occ_n] = occ_energy[...]
            blocks[d][c, n : n + 1, occ_n:n] = emp_energy[...]


def gate_kernel(waits, *refs):
    pieces, out = refs[: -1 - waits], refs[-1]
    for s, piece in enumerate(pieces):
        out[s] = piece[0 : out.shape[1], :]


def scale_kernel(chunk, T, C, counts, *refs):
    occ_r, emp_r = counts
    n = occ_r + emp_r
    place, rows, (s_high, s_low, flat, falls) = refs[0], refs[1:3], refs[-4:]
    instant, slots = refs[3 : 3 + T], rows[0].shape[0]
    k_occ = occ_r * slots * C
    q = place[2]
    breadth = flat.shape[1]
    lane = lax.broadcasted_iota(jnp.int32, (1, breadth), 1)
    instants = jnp.zeros((1, breadth), f32)
    for t in range(T):
        instants = jnp.where(lane == t, instant[t][-1:, 0:1], instants)
    for s in range(slots):
        for core in range(2):
            for d in range(C // 2):
                at = s * C + (q ^ (2 * d + core))
                block = rows[core].at[s, d]
                occ_at = pl.ds(pl.multiple_of(at * occ_r, 8), occ_r)
                emp_at = pl.ds(pl.multiple_of(k_occ + at * emp_r, 8), emp_r)
                flat[occ_at, :] = block[chunk, 0:occ_r, :]
                flat[emp_at, :] = block[chunk, occ_r:n, :]
                levels = block[chunk, n : n + EXTRA, :].T[0:n, 0:1]
                decay = jnp.exp(-(levels * instants))
                falls[occ_at, :] = decay[0:occ_r]
                falls[emp_at, :] = decay[occ_r:n]
    step = 128
    for at in range(0, flat.shape[0], step):
        turned = flat[at : at + step, :].T
        decay = falls[at : at + step, :].T
        for t in range(T):
            high, low = split(turned * decay[t : t + 1, :])
            s_high[t * breadth : (t + 1) * breadth, at : at + step] = high
            s_low[t * breadth : (t + 1) * breadth, at : at + step] = low


def halves_kernel(slots, C, X, counts, waits, *refs):
    occ_c, emp_c = counts
    place, cols = refs[0], refs[1 : 1 + len(slots)]
    high, low, columns = refs[1 + len(slots) + waits :]
    x, q, piece = place[1], place[2], cols[0].shape[-1]
    size = columns.shape[0] // (X * (occ_c + emp_c))
    k_occ = occ_c * X * size
    for part, where in enumerate(slots):
        for i, (dx, dq, s) in enumerate(where):
            lanes = slice((dq // 2) * piece, (dq // 2) * piece + piece)
            at = s * X + (x ^ dx)
            columns[pl.ds(pl.multiple_of(at * occ_c, 8), occ_c), lanes] = cols[part][i, 0:occ_c, :]
            columns[pl.ds(pl.multiple_of(k_occ + at * emp_c, 8), emp_c), lanes] = cols[part][i, occ_c : occ_c + emp_c, :]
    line = lax.broadcasted_iota(jnp.int32, (piece, piece), 0)
    lane = lax.broadcasted_iota(jnp.int32, (piece, piece), 1)
    for d in range(C // 2):
        lanes = slice(d * piece, (d + 1) * piece)
        goal = jnp.where((q ^ (2 * d)) >= C // 2, piece - 1 - lane, lane)
        turn = jnp.where(line == goal, 1.0, 0.0).astype(bf16)
        a, b = split(columns[:, lanes])
        high[:, lanes] = dot(a, turn).astype(bf16)
        low[:, lanes] = dot(b, turn).astype(bf16)


def green_kernel(T, groups, k_occ, *refs):
    place, weights = refs[:2]
    scaled, halves, outs = refs[2 : 2 + 2 * groups], refs[2 + 2 * groups : -T], refs[-T:]
    k, breadth = place[0], outs[0].shape[0]

    def green(lines):
        total = None
        for g in range(groups):
            a_high, a_low = scaled[2 * g][:, lines], scaled[2 * g + 1][:, lines]
            c_high, c_low = halves[2 * g][lines, :], halves[2 * g + 1][lines, :]
            term = dot(a_high, c_high) + dot(a_high, c_low) + dot(a_low, c_high)
            total = term if total is None else total + term
        return total

    product = green(slice(0, k_occ)) * green(slice(k_occ, scaled[0].shape[1]))
    for w in range(T):
        total = weights[k ^ w, k] * product[0:breadth, :]
        for t in range(1, T):
            total += weights[k ^ w, k ^ t] * product[t * breadth : (t + 1) * breadth, :]
        outs[w][...] = total


def token_kernel(_, out):
    out[...] = jnp.zeros_like(out)


def pack_kernel(order, *refs):
    for i, s in enumerate(order):
        refs[-1][s] = refs[i][...]


def cost(us):
    return pl.CostEstimate(flops=int(us * 1e9), bytes_accessed=0, transcendentals=0)


def table_kernel(near, far, high, low):
    share = far.shape[1]
    for h in range(share):
        c, s = far[0, h : h + 1, :], far[1, h : h + 1, :]
        for odd in range(2):
            value = c * near[2 * odd] - s * near[2 * odd + 1]
            a, b = split(value)
            high[odd, h * FINE : (h + 1) * FINE, :] = a
            low[odd, h * FINE : (h + 1) * FINE, :] = b


def fold_kernel(block, groups, waits, high, low, *refs):
    here, there = refs[:2]
    out, both = refs[2 + waits :]
    T, breadth, width = here.shape
    step = width // groups
    at = 0
    for s in range(T):
        for d in range(groups):
            mine = here[s, :, d * step : (d + 1) * step]
            e = groups - 1 - d
            theirs = there[s ^ (T - 1), :, e * step : (e + 1) * step]
            for odd, value in enumerate((mine + theirs, mine - theirs)):
                a, b = split(value.T)
                both[odd, at : at + step, 0:breadth] = a
                both[odd, at : at + step, breadth:] = b
            at += step
    mode_kernel(block, 0, high, low, both, out)


def mode_kernel(block, waits, high, low, both, *refs):
    out = refs[-1]
    share, breadth = out.shape[0] // 2, out.shape[1]
    lines = slice(block * share, (block + 1) * share)
    for odd in range(2):
        twice = dot(high[odd, lines, :], both[odd])
        once = dot(low[odd, lines, :], both[odd, :, 0:breadth])
        out[pl.ds(odd, share, stride=2), :] = twice[:, :breadth] + twice[:, breadth:] + once


def place_kernel(first, place, *refs):
    pieces, out, done = refs[:-2], refs[-2], refs[-1]
    copies = []
    for i, (chunk, d) in enumerate(first):
        breadth = pieces[i].shape[1]
        at = ((place[2] // 2) ^ d) * CHUNKS + chunk
        copies.append(pltpu.make_async_copy(pieces[i], out.at[0, :, pl.ds(pl.multiple_of(at * breadth, breadth), breadth)], done.at[i]))
    for copy in copies:
        copy.start()
    for copy in copies:
        copy.wait()


def per_device(occ_rows, emp_rows, occ_cols, emp_cols, occ_energy, emp_energy, times, freq_weight):
    T, X, C = lax.axis_size("tm"), lax.axis_size("row"), lax.axis_size("col")
    k, x, q = lax.axis_index("tm"), lax.axis_index("row"), lax.axis_index("col")
    number_rows, number_cols = occ_rows.shape[0], occ_cols.shape[0]
    occ_r, emp_r, occ_c, emp_c = (a.shape[1] for a in (occ_rows, emp_rows, occ_cols, emp_cols))
    n, m = occ_r + emp_r, occ_c + emp_c
    H = C // 2
    rp, jp = number_rows // (H * CHUNKS), number_cols // T
    k_occ, k_emp = occ_r * T * C, emp_r * T * C
    high_bits = [("col", b) for b in bits_of(C) if b > 1]
    row_bits = [("row", b) for b in bits_of(X)]

    place = jnp.stack([k, x, q]).astype(jnp.int32)
    smem = pl.BlockSpec(memory_space=pltpu.SMEM)
    vmem = pl.BlockSpec(memory_space=pltpu.VMEM)
    hbm = pl.BlockSpec(memory_space=pl.ANY)
    params = pltpu.CompilerParams(vmem_limit_bytes=VMEM_LIMIT)

    sources = [occ_cols.T, emp_cols.T, occ_rows.T, emp_rows.T, occ_energy, emp_energy]
    prepared = pl.pallas_call(
        functools.partial(prepare_kernel, T, H),
        out_shape=[jax.ShapeDtypeStruct((m + EXTRA, jp), f32)] * T + [jax.ShapeDtypeStruct((CHUNKS, n + EXTRA, rp), f32)] * H,
        in_specs=[smem] + [hbm] * len(sources),
        out_specs=[vmem] * (T + H),
        scratch_shapes=[pltpu.VMEM(a.shape, f32) for a in sources] + [pltpu.SemaphoreType.DMA((len(sources),))],
        compiler_params=pltpu.CompilerParams(vmem_limit_bytes=VMEM_ALL),
        cost_estimate=cost(0),
        name="prepare",
    )(times, *sources)
    pieces, row_pieces = prepared[:T], prepared[T:]
    col_slots = [pieces[0]] + [swap(pieces[s], "tm", s) for s in range(1, T)]
    own_rows = jnp.stack([row_pieces[0]] + [swap(row_pieces[d], "col", 2 * d) for d in range(1, H)])
    got_rows = {0: own_rows}
    for bit in bits_of(T):
        for s in list(got_rows):
            got_rows[s ^ bit] = swap(got_rows[s], "tm", bit)
    early_rows = jnp.stack([got_rows[s] for s in range(T // 2)])
    row_slots = [[early_rows, swap(early_rows, "col", 1)]]

    groups = [list(range(T))[: T // 2], list(range(T))[T // 2 :]]
    cuts = [[groups[0]], [groups[1][: T // 4], groups[1][T // 4 :]]]
    orders = [[row_bits + high_bits], [row_bits + high_bits, high_bits + row_bits]]
    cols, slots, firsts = [], [], []
    for group, parts, ways in zip(groups, cuts, orders):
        there, where = [], []
        for part, order in zip(parts, ways):
            waits = firsts[:1] if GATE and group is groups[1] else []
            value = pl.pallas_call(
                functools.partial(gate_kernel, len(waits)),
                out_shape=jax.ShapeDtypeStruct((len(part), m, jp), f32),
                in_specs=[vmem] * len(part) + [hbm] * len(waits),
                out_specs=vmem,
                compiler_params=params,
                cost_estimate=cost(0),
                name="gate",
            )(*[col_slots[s] for s in part], *waits)
            values = [(value, [(0, 0, group.index(s)) for s in part])]
            for axis, bit in order:
                if len(values) > 1:
                    values = [(jnp.concatenate([v for v, _ in values], 0), sum((w for _, w in values), []))]
                value, at = values[0]
                far = [(dx ^ bit, dq, f) if axis == "row" else (dx, dq ^ bit, f) for dx, dq, f in at]
                values.append((swap(value, axis, bit), far))
                firsts.append(values[-1][0])
            there += [v for v, _ in values]
            where += [w for _, w in values]
        cols.append(there)
        slots.append(where)

    wide = H * jp

    slot = jnp.arange(T, dtype=jnp.int32)[:, None, None]
    dq = 2 * jnp.arange(H, dtype=jnp.int32)[None, :, None]
    inner = jnp.arange(jp, dtype=jnp.int32)[None, None, :]
    source = q ^ dq
    lane = jnp.where(source >= C // 2, jp - 1 - inner, inner)
    column = (source * number_cols + (k ^ slot) * jp + lane).reshape(-1)
    odd_column = 2 * column + 1
    share = GP // C

    def angle(wave):
        phase = (odd_column[None, :] * wave[:, None]) % (4 * GP)
        return jnp.pi * phase.astype(f32) / (2.0 * GP)

    scale = jnp.sqrt(2.0 / GP)
    fine = 2 * jnp.arange(FINE, dtype=jnp.int32)
    per_block = share // (2 * FINE)
    blocks = q ^ (2 * jnp.arange(H, dtype=jnp.int32)[::-1])
    coarse = (blocks[:, None] * share + 2 * FINE * jnp.arange(per_block, dtype=jnp.int32)[None, :]).reshape(-1)
    even, odd, far = angle(fine), angle(fine + 1), angle(coarse)
    near = jnp.stack([scale * jnp.cos(even), scale * jnp.sin(even), scale * jnp.cos(odd), scale * jnp.sin(odd)])
    far = jnp.stack([jnp.cos(far), jnp.sin(far)])
    all_cols = T * wide
    t_high, t_low = pl.pallas_call(
        table_kernel,
        out_shape=[jax.ShapeDtypeStruct((2, H * share // 2, all_cols), bf16)] * 2,
        in_specs=[pl.BlockSpec()] * 2,
        out_specs=[vmem] * 2,
        compiler_params=params,
        cost_estimate=cost(0),
        name="cosines",
    )(near, far)

    halves, waits = [], [t_high]
    for g, group in enumerate(groups):
        got = pl.pallas_call(
            functools.partial(halves_kernel, slots[g], C, X, (occ_c, emp_c), len(waits)),
            out_shape=[jax.ShapeDtypeStruct(((k_occ + k_emp) // len(groups), wide), bf16)] * 2,
            in_specs=[smem] + [pl.BlockSpec()] * len(cols[g]) + [hbm] * len(waits),
            out_specs=[vmem] * 2,
            scratch_shapes=[pltpu.VMEM(((k_occ + k_emp) // len(groups), wide), f32)],
            compiler_params=params,
            cost_estimate=cost(HALVES_COST[g]),
            name="halves",
        )(place, *cols[g], *waits)
        halves += got
        waits = [got[0]]

    own, instants = [], [slot[-EXTRA:] for slot in col_slots]
    for chunk in range(CHUNKS):
        scaled = []
        for g in range(len(groups)):
            if len(row_slots) == g:
                late_rows = pl.pallas_call(
                    functools.partial(pack_kernel, range(T // 2)),
                    out_shape=jax.ShapeDtypeStruct(early_rows.shape, f32),
                    in_specs=[vmem] * (T // 2) + [hbm] * 2,
                    out_specs=vmem,
                    compiler_params=params,
                    cost_estimate=cost(0),
                    name="pack",
                )(*[got_rows[s] for s in groups[g]], scaled[0], halves[0])
                row_slots.append([late_rows, swap(late_rows, "col", 1)])
            k_group = (k_occ + k_emp) // len(groups)
            scaled += pl.pallas_call(
                functools.partial(scale_kernel, chunk, T, C, (occ_r, emp_r)),
                out_shape=[jax.ShapeDtypeStruct((T * rp, k_group), bf16)] * 2,
                in_specs=[smem] + [pl.BlockSpec()] * 2 + [vmem] * T + [hbm] * len(own),
                out_specs=[vmem] * 2,
                scratch_shapes=[pltpu.VMEM((k_group, rp), f32)] * 2,
                compiler_params=params,
                cost_estimate=cost(SCALE_COST[g]),
                name="scale",
            )(place, *row_slots[g], *instants, *[here[0] for here in own])
        series = pl.pallas_call(
            functools.partial(green_kernel, T, len(groups), k_occ // len(groups)),
            out_shape=[jax.ShapeDtypeStruct((rp, wide), f32)] * T,
            in_specs=[smem, smem] + [vmem] * (len(scaled) + len(halves)),
            out_specs=[vmem] * T,
            compiler_params=params,
            cost_estimate=cost(GREENS_COST),
            name="greens",
        )(place, freq_weight, *scaled, *halves)
        here = [series[0]] + [None] * (T - 1)
        for s in range(T - 1, 0, -1):
            here[s] = swap(series[s], "tm", s)
        own.append(here)

    def assemble(parts, before):
        return pl.pallas_call(
            functools.partial(place_kernel, [at for at, _ in parts]),
            out_shape=jax.ShapeDtypeStruct((1, share, number_rows), f32),
            in_specs=[smem] + [hbm] * (len(parts) + len(before)),
            out_specs=hbm,
            scratch_shapes=[pltpu.SemaphoreType.DMA((len(parts),))],
            input_output_aliases={1 + len(parts): 0} if before else {},
            compiler_params=params,
            cost_estimate=cost(0),
            name="assemble",
        )(place, *[part for _, part in parts], *before)

    early, late = [], []
    for chunk in range(CHUNKS):
        behind = [own[chunk + 1][BEHIND]] if chunk + 1 < CHUNKS else []
        mine = pl.pallas_call(
            functools.partial(pack_kernel, range(T)),
            out_shape=jax.ShapeDtypeStruct((T, rp, wide), f32),
            in_specs=[vmem] * T + [hbm] * len(behind),
            out_specs=vmem,
            compiler_params=params,
            cost_estimate=cost(0),
            name="pack",
        )(*own[chunk], *behind)
        waits = [
            pl.pallas_call(
                token_kernel,
                out_shape=jax.ShapeDtypeStruct((8, 128), f32),
                in_specs=[hbm],
                compiler_params=params,
                cost_estimate=cost(TOKEN_COST),
                name="token",
            )(part)
            for _, part in late
        ]
        shape = jax.ShapeDtypeStruct((share, rp), f32)
        made = pl.pallas_call(
            functools.partial(fold_kernel, 0, H, len(waits)),
            out_shape=[shape, jax.ShapeDtypeStruct((2, all_cols, 2 * rp), bf16)],
            in_specs=[vmem] * 4 + [hbm] * len(waits),
            out_specs=[vmem] * 2,
            compiler_params=params,
            cost_estimate=cost(0),
            name="modes",
        )(t_high, t_low, mine, swap(mine, "col", 1), *waits)
        made, both = [made[0]], made[1]
        for block in range(1, H):
            made.append(
                pl.pallas_call(
                    functools.partial(mode_kernel, block, 0),
                    out_shape=shape,
                    in_specs=[vmem] * 3,
                    out_specs=vmem,
                    compiler_params=params,
                    cost_estimate=cost(0),
                    name="modes",
                )(t_high, t_low, both)
            )
        early = early + late + [((chunk, 0), made[H - 1])]
        late = [((chunk, d), swap(made[H - 1 - d], "col", 2 * d)) for d in range(1, H)]
    return assemble(late, [assemble(early, [])])


def solution(mesh):
    return jax.shard_map(
        per_device,
        mesh=mesh,
        in_specs=(
            P("row", ("tm", "col")),
            P("row", ("tm", "col")),
            P("col", ("tm", "row")),
            P("col", ("tm", "row")),
            P(None, ("tm", "col")),
            P(None, ("tm", "col")),
            P("tm"),
            P(),
        ),
        out_specs=P("tm", "col", "row"),
        check_vma=False,
    )
```

```python
import functools

import jax
import jax.numpy as jnp
from jax import lax
from jax.experimental import pallas as pl
from jax.experimental.pallas import tpu as pltpu
from jax.sharding import PartitionSpec as P

GP = 2048
f32, bf16 = jnp.float32, jnp.bfloat16
VMEM_LIMIT = 32 * 1024 * 1024
VMEM_ALL = 60 * 1024 * 1024
EXTRA = 8
CHUNKS = 2
FINE = 32
HALVES_COST, SCALE_COST, GREENS_COST, TOKEN_COST, BEHIND, GATE, PARTS = (12, 8), (0, 0), 3, 0.7, 1, 1, 1


def bits_of(size):
    return [1 << b for b in range(size.bit_length() - 1)][::-1]


def swap(value, axis, bit):
    size = lax.axis_size(axis)
    return lax.ppermute(value, axis, [(i, i ^ bit) for i in range(size)])


def split(value):
    high = value.astype(bf16)
    return high, (value - high.astype(f32)).astype(bf16)


def dot(a, b):
    return lax.dot_general(a, b, (((1,), (0,)), ((), ())), preferred_element_type=f32)


def prepare_kernel(T, H, times, *refs):
    sources, slices, blocks = refs[:6], refs[6 : 6 + T], refs[6 + T : 6 + T + H]
    here, done = refs[6 + T + H : -1], refs[-1]
    copies = [pltpu.make_async_copy(a, b, done.at[i]) for i, (a, b) in enumerate(zip(sources, here))]
    for copy in copies:
        copy.start()
    for copy in copies:
        copy.wait()
    occ_c, emp_c, occ_r, emp_r, occ_energy, emp_energy = here
    k, q = lax.axis_index("tm"), lax.axis_index("col")
    n, piece = occ_c.shape[0], slices[0].shape[1]
    for s in range(T):
        for one in range(T) if piece % 128 else (None,):
            @pl.when(True if one is None else (k ^ s) == one)
            def _():
                first = pl.multiple_of((k ^ s) * piece, piece) if one is None else one * piece
                slices[s][0:n, :] = occ_c[:, pl.ds(first, piece)]
                slices[s][n:-EXTRA, :] = emp_c[:, pl.ds(first, piece)]
        slices[s][-EXTRA:, :] = jnp.full((EXTRA, piece), times[0], f32)
    chunks, lines, breadth = blocks[0].shape
    occ_n, n = occ_r.shape[0], lines - EXTRA
    for d in range(H):
        for c in range(chunks):
            first = (((q // 2) ^ d) * chunks + c) * breadth
            at = pl.ds(pl.multiple_of(first, breadth), breadth)
            blocks[d][c, 0:occ_n, :] = occ_r[:, at]
            blocks[d][c, occ_n:n, :] = emp_r[:, at]
            blocks[d][c, n:, :] = jnp.zeros((EXTRA, breadth), f32)
            blocks[d][c, n : n + 1, 0:occ_n] = occ_energy[...]
            blocks[d][c, n : n + 1, occ_n:n] = emp_energy[...]


def gate_kernel(waits, *refs):
    pieces, out = refs[: -1 - waits], refs[-1]
    for s, piece in enumerate(pieces):
        out[s] = piece[0 : out.shape[1], :]


def scale_kernel(chunk, T, C, counts, *refs):
    occ_r, emp_r = counts
    n = occ_r + emp_r
    place, rows, (s_high, s_low, flat, falls) = refs[0], refs[1:3], refs[-4:]
    instant, slots = refs[3 : 3 + T], rows[0].shape[0]
    k_occ = occ_r * slots * C
    q = place[2]
    breadth = flat.shape[1]
    lane = lax.broadcasted_iota(jnp.int32, (1, breadth), 1)
    instants = jnp.zeros((1, breadth), f32)
    for t in range(T):
        instants = jnp.where(lane == t, instant[t][-1:, 0:1], instants)
    for s in range(slots):
        for core in range(2):
            for d in range(C // 2):
                at = s * C + (q ^ (2 * d + core))
                block = rows[core].at[s, d]
                occ_at = pl.ds(pl.multiple_of(at * occ_r, 8), occ_r)
                emp_at = pl.ds(pl.multiple_of(k_occ + at * emp_r, 8), emp_r)
                flat[occ_at, :] = block[chunk, 0:occ_r, :]
                flat[emp_at, :] = block[chunk, occ_r:n, :]
                levels = block[chunk, n : n + EXTRA, :].T[0:n, 0:1]
                decay = jnp.exp(-(levels * instants))
                falls[occ_at, :] = decay[0:occ_r]
                falls[emp_at, :] = decay[occ_r:n]
    step = 128
    for at in range(0, flat.shape[0], step):
        turned = flat[at : at + step, :].T
        decay = falls[at : at + step, :].T
        for t in range(T):
            high, low = split(turned * decay[t : t + 1, :])
            s_high[t * breadth : (t + 1) * breadth, at : at + step] = high
            s_low[t * breadth : (t + 1) * breadth, at : at + step] = low


def halves_kernel(slots, C, X, counts, waits, *refs):
    occ_c, emp_c = counts
    place, cols = refs[0], refs[1 : 1 + len(slots)]
    high, low, columns = refs[1 + len(slots) + waits :]
    x, q, piece = place[1], place[2], cols[0].shape[-1]
    size = columns.shape[0] // (X * (occ_c + emp_c))
    k_occ = occ_c * X * size
    for part, where in enumerate(slots):
        for i, (dx, dq, s) in enumerate(where):
            lanes = slice((dq // 2) * piece, (dq // 2) * piece + piece)
            at = s * X + (x ^ dx)
            columns[pl.ds(pl.multiple_of(at * occ_c, 8), occ_c), lanes] = cols[part][i, 0:occ_c, :]
            columns[pl.ds(pl.multiple_of(k_occ + at * emp_c, 8), emp_c), lanes] = cols[part][i, occ_c : occ_c + emp_c, :]
    line = lax.broadcasted_iota(jnp.int32, (piece, piece), 0)
    lane = lax.broadcasted_iota(jnp.int32, (piece, piece), 1)
    for d in range(C // 2):
        lanes = slice(d * piece, (d + 1) * piece)
        goal = jnp.where((q ^ (2 * d)) >= C // 2, piece - 1 - lane, lane)
        turn = jnp.where(line == goal, 1.0, 0.0).astype(bf16)
        a, b = split(columns[:, lanes])
        high[:, lanes] = dot(a, turn).astype(bf16)
        low[:, lanes] = dot(b, turn).astype(bf16)


def green_kernel(T, groups, k_occ, *refs):
    place, weights = refs[:2]
    scaled, halves, outs = refs[2 : 2 + 2 * groups], refs[2 + 2 * groups : -T], refs[-T:]
    k, breadth = place[0], outs[0].shape[0]

    def green(lines):
        total = None
        for g in range(groups):
            a_high, a_low = scaled[2 * g][:, lines], scaled[2 * g + 1][:, lines]
            c_high, c_low = halves[2 * g][lines, :], halves[2 * g + 1][lines, :]
            term = dot(a_high, c_high) + dot(a_high, c_low) + dot(a_low, c_high)
            total = term if total is None else total + term
        return total

    product = green(slice(0, k_occ)) * green(slice(k_occ, scaled[0].shape[1]))
    for w in range(T):
        total = weights[k ^ w, k] * product[0:breadth, :]
        for t in range(1, T):
            total += weights[k ^ w, k ^ t] * product[t * breadth : (t + 1) * breadth, :]
        outs[w][...] = total


def token_kernel(_, out):
    out[...] = jnp.zeros_like(out)


def pack_kernel(order, *refs):
    for i, s in enumerate(order):
        refs[-1][s] = refs[i][...]


def cost(us):
    return pl.CostEstimate(flops=int(us * 1e9), bytes_accessed=0, transcendentals=0)


def table_kernel(near, far, high, low):
    share = far.shape[1]
    for h in range(share):
        c, s = far[0, h : h + 1, :], far[1, h : h + 1, :]
        for odd in range(2):
            value = c * near[2 * odd] - s * near[2 * odd + 1]
            a, b = split(value)
            high[odd, h * FINE : (h + 1) * FINE, :] = a
            low[odd, h * FINE : (h + 1) * FINE, :] = b


def fold_kernel(block, groups, packs, waits, high, low, *refs):
    here = [refs[2 * i].at[s] for i in range(packs) for s in range(refs[2 * i].shape[0])]
    there = [refs[2 * i + 1].at[s] for i in range(packs) for s in range(refs[2 * i + 1].shape[0])]
    out, both = refs[2 * packs + waits :]
    T, (breadth, width) = len(here), here[0].shape
    step = width // groups
    at = 0
    for s in range(T):
        for d in range(groups):
            mine = here[s][:, d * step : (d + 1) * step]
            e = groups - 1 - d
            theirs = there[s ^ (T - 1)][:, e * step : (e + 1) * step]
            for odd, value in enumerate((mine + theirs, mine - theirs)):
                a, b = split(value.T)
                both[odd, at : at + step, 0:breadth] = a
                both[odd, at : at + step, breadth:] = b
            at += step
    mode_kernel(block, 0, high, low, both, out)


def mode_kernel(block, waits, high, low, both, *refs):
    out = refs[-1]
    share, breadth = out.shape[0] // 2, out.shape[1]
    lines = slice(block * share, (block + 1) * share)
    for odd in range(2):
        twice = dot(high[odd, lines, :], both[odd])
        once = dot(low[odd, lines, :], both[odd, :, 0:breadth])
        out[pl.ds(odd, share, stride=2), :] = twice[:, :breadth] + twice[:, breadth:] + once


def place_kernel(first, place, *refs):
    pieces, out, done = refs[:-2], refs[-2], refs[-1]
    copies = []
    for i, (chunk, d) in enumerate(first):
        breadth = pieces[i].shape[1]
        at = ((place[2] // 2) ^ d) * CHUNKS + chunk
        copies.append(pltpu.make_async_copy(pieces[i], out.at[0, :, pl.ds(pl.multiple_of(at * breadth, breadth), breadth)], done.at[i]))
    for copy in copies:
        copy.start()
    for copy in copies:
        copy.wait()


def per_device(occ_rows, emp_rows, occ_cols, emp_cols, occ_energy, emp_energy, times, freq_weight):
    T, X, C = lax.axis_size("tm"), lax.axis_size("row"), lax.axis_size("col")
    k, x, q = lax.axis_index("tm"), lax.axis_index("row"), lax.axis_index("col")
    number_rows, number_cols = occ_rows.shape[0], occ_cols.shape[0]
    occ_r, emp_r, occ_c, emp_c = (a.shape[1] for a in (occ_rows, emp_rows, occ_cols, emp_cols))
    n, m = occ_r + emp_r, occ_c + emp_c
    H = C // 2
    rp, jp = number_rows // (H * CHUNKS), number_cols // T
    k_occ, k_emp = occ_r * T * C, emp_r * T * C
    high_bits = [("col", b) for b in bits_of(C) if b > 1]
    row_bits = [("row", b) for b in bits_of(X)]

    place = jnp.stack([k, x, q]).astype(jnp.int32)
    smem = pl.BlockSpec(memory_space=pltpu.SMEM)
    vmem = pl.BlockSpec(memory_space=pltpu.VMEM)
    hbm = pl.BlockSpec(memory_space=pl.ANY)
    params = pltpu.CompilerParams(vmem_limit_bytes=VMEM_LIMIT)

    sources = [occ_cols.T, emp_cols.T, occ_rows.T, emp_rows.T, occ_energy, emp_energy]
    prepared = pl.pallas_call(
        functools.partial(prepare_kernel, T, H),
        out_shape=[jax.ShapeDtypeStruct((m + EXTRA, jp), f32)] * T + [jax.ShapeDtypeStruct((CHUNKS, n + EXTRA, rp), f32)] * H,
        in_specs=[smem] + [hbm] * len(sources),
        out_specs=[vmem] * (T + H),
        scratch_shapes=[pltpu.VMEM(a.shape, f32) for a in sources] + [pltpu.SemaphoreType.DMA((len(sources),))],
        compiler_params=pltpu.CompilerParams(vmem_limit_bytes=VMEM_ALL),
        cost_estimate=cost(0),
        name="prepare",
    )(times, *sources)
    pieces, row_pieces = prepared[:T], prepared[T:]
    col_slots = [pieces[0]] + [swap(pieces[s], "tm", s) for s in range(1, T)]
    own_rows = jnp.stack([row_pieces[0]] + [swap(row_pieces[d], "col", 2 * d) for d in range(1, H)])
    got_rows = {0: own_rows}
    for bit in bits_of(T):
        for s in list(got_rows):
            got_rows[s ^ bit] = swap(got_rows[s], "tm", bit)
    early_rows = jnp.stack([got_rows[s] for s in range(T // 2)])
    row_slots = [[early_rows, swap(early_rows, "col", 1)]]

    groups = [list(range(T))[: T // 2], list(range(T))[T // 2 :]]
    cuts = [[groups[0]], [groups[1][: T // 4], groups[1][T // 4 :]]]
    orders = [[row_bits + high_bits], [row_bits + high_bits, high_bits + row_bits]]
    cols, slots, firsts = [], [], []
    for group, parts, ways in zip(groups, cuts, orders):
        there, where = [], []
        for part, order in zip(parts, ways):
            waits = firsts[:1] if GATE and group is groups[1] else []
            value = pl.pallas_call(
                functools.partial(gate_kernel, len(waits)),
                out_shape=jax.ShapeDtypeStruct((len(part), m, jp), f32),
                in_specs=[vmem] * len(part) + [hbm] * len(waits),
                out_specs=vmem,
                compiler_params=params,
                cost_estimate=cost(0),
                name="gate",
            )(*[col_slots[s] for s in part], *waits)
            values = [(value, [(0, 0, group.index(s)) for s in part])]
            for axis, bit in order:
                if len(values) > 1:
                    values = [(jnp.concatenate([v for v, _ in values], 0), sum((w for _, w in values), []))]
                value, at = values[0]
                far = [(dx ^ bit, dq, f) if axis == "row" else (dx, dq ^ bit, f) for dx, dq, f in at]
                values.append((swap(value, axis, bit), far))
                firsts.append(values[-1][0])
            there += [v for v, _ in values]
            where += [w for _, w in values]
        cols.append(there)
        slots.append(where)

    wide = H * jp

    slot = jnp.arange(T, dtype=jnp.int32)[:, None, None]
    dq = 2 * jnp.arange(H, dtype=jnp.int32)[None, :, None]
    inner = jnp.arange(jp, dtype=jnp.int32)[None, None, :]
    source = q ^ dq
    lane = jnp.where(source >= C // 2, jp - 1 - inner, inner)
    column = (source * number_cols + (k ^ slot) * jp + lane).reshape(-1)
    odd_column = 2 * column + 1
    share = GP // C

    def angle(wave):
        phase = (odd_column[None, :] * wave[:, None]) % (4 * GP)
        return jnp.pi * phase.astype(f32) / (2.0 * GP)

    scale = jnp.sqrt(2.0 / GP)
    fine = 2 * jnp.arange(FINE, dtype=jnp.int32)
    per_block = share // (2 * FINE)
    blocks = q ^ (2 * jnp.arange(H, dtype=jnp.int32)[::-1])
    coarse = (blocks[:, None] * share + 2 * FINE * jnp.arange(per_block, dtype=jnp.int32)[None, :]).reshape(-1)
    even, odd, far = angle(fine), angle(fine + 1), angle(coarse)
    near = jnp.stack([scale * jnp.cos(even), scale * jnp.sin(even), scale * jnp.cos(odd), scale * jnp.sin(odd)])
    far = jnp.stack([jnp.cos(far), jnp.sin(far)])
    all_cols = T * wide
    t_high, t_low = pl.pallas_call(
        table_kernel,
        out_shape=[jax.ShapeDtypeStruct((2, H * share // 2, all_cols), bf16)] * 2,
        in_specs=[pl.BlockSpec()] * 2,
        out_specs=[vmem] * 2,
        compiler_params=params,
        cost_estimate=cost(0),
        name="cosines",
    )(near, far)

    halves, waits = [], [t_high]
    for g, group in enumerate(groups):
        got = pl.pallas_call(
            functools.partial(halves_kernel, slots[g], C, X, (occ_c, emp_c), len(waits)),
            out_shape=[jax.ShapeDtypeStruct(((k_occ + k_emp) // len(groups), wide), bf16)] * 2,
            in_specs=[smem] + [pl.BlockSpec()] * len(cols[g]) + [hbm] * len(waits),
            out_specs=[vmem] * 2,
            scratch_shapes=[pltpu.VMEM(((k_occ + k_emp) // len(groups), wide), f32)],
            compiler_params=params,
            cost_estimate=cost(HALVES_COST[g]),
            name="halves",
        )(place, *cols[g], *waits)
        halves += got
        waits = [got[0]]

    own, instants = [], [slot[-EXTRA:] for slot in col_slots]
    for chunk in range(CHUNKS):
        scaled = []
        for g in range(len(groups)):
            if len(row_slots) == g:
                late_rows = pl.pallas_call(
                    functools.partial(pack_kernel, range(T // 2)),
                    out_shape=jax.ShapeDtypeStruct(early_rows.shape, f32),
                    in_specs=[vmem] * (T // 2) + [hbm] * 2,
                    out_specs=vmem,
                    compiler_params=params,
                    cost_estimate=cost(0),
                    name="pack",
                )(*[got_rows[s] for s in groups[g]], scaled[0], halves[0])
                row_slots.append([late_rows, swap(late_rows, "col", 1)])
            k_group = (k_occ + k_emp) // len(groups)
            scaled += pl.pallas_call(
                functools.partial(scale_kernel, chunk, T, C, (occ_r, emp_r)),
                out_shape=[jax.ShapeDtypeStruct((T * rp, k_group), bf16)] * 2,
                in_specs=[smem] + [pl.BlockSpec()] * 2 + [vmem] * T + [hbm] * len(own),
                out_specs=[vmem] * 2,
                scratch_shapes=[pltpu.VMEM((k_group, rp), f32)] * 2,
                compiler_params=params,
                cost_estimate=cost(SCALE_COST[g]),
                name="scale",
            )(place, *row_slots[g], *instants, *[here[0] for here in own])
        series = pl.pallas_call(
            functools.partial(green_kernel, T, len(groups), k_occ // len(groups)),
            out_shape=[jax.ShapeDtypeStruct((rp, wide), f32)] * T,
            in_specs=[smem, smem] + [vmem] * (len(scaled) + len(halves)),
            out_specs=[vmem] * T,
            compiler_params=params,
            cost_estimate=cost(GREENS_COST),
            name="greens",
        )(place, freq_weight, *scaled, *halves)
        here = [series[0]] + [None] * (T - 1)
        for s in range(T - 1, 0, -1):
            here[s] = swap(series[s], "tm", s)
        own.append(here)

    def assemble(parts, before):
        return pl.pallas_call(
            functools.partial(place_kernel, [at for at, _ in parts]),
            out_shape=jax.ShapeDtypeStruct((1, share, number_rows), f32),
            in_specs=[smem] + [hbm] * (len(parts) + len(before)),
            out_specs=hbm,
            scratch_shapes=[pltpu.SemaphoreType.DMA((len(parts),))],
            input_output_aliases={1 + len(parts): 0} if before else {},
            compiler_params=params,
            cost_estimate=cost(0),
            name="assemble",
        )(place, *[part for _, part in parts], *before)

    early, late = [], []
    for chunk in range(CHUNKS):
        behind = [own[chunk + 1][BEHIND]] if chunk + 1 < CHUNKS else []
        packed = []
        for group in groups if PARTS and chunk == CHUNKS - 1 else [range(T)]:
            mine = pl.pallas_call(
                functools.partial(pack_kernel, range(len(group))),
                out_shape=jax.ShapeDtypeStruct((len(group), rp, wide), f32),
                in_specs=[vmem] * len(group) + [hbm] * len(behind),
                out_specs=vmem,
                compiler_params=params,
                cost_estimate=cost(0),
                name="pack",
            )(*[own[chunk][s] for s in group], *behind)
            packed += [mine, swap(mine, "col", 1)]
            behind = packed[-1:]
        waits = [
            pl.pallas_call(
                token_kernel,
                out_shape=jax.ShapeDtypeStruct((8, 128), f32),
                in_specs=[hbm],
                compiler_params=params,
                cost_estimate=cost(TOKEN_COST),
                name="token",
            )(part)
            for _, part in late
        ]
        shape = jax.ShapeDtypeStruct((share, rp), f32)
        made = pl.pallas_call(
            functools.partial(fold_kernel, 0, H, len(packed) // 2, len(waits)),
            out_shape=[shape, jax.ShapeDtypeStruct((2, all_cols, 2 * rp), bf16)],
            in_specs=[vmem] * (2 + len(packed)) + [hbm] * len(waits),
            out_specs=[vmem] * 2,
            compiler_params=params,
            cost_estimate=cost(0),
            name="modes",
        )(t_high, t_low, *packed, *waits)
        made, both = [made[0]], made[1]
        for block in range(1, H):
            made.append(
                pl.pallas_call(
                    functools.partial(mode_kernel, block, 0),
                    out_shape=shape,
                    in_specs=[vmem] * 3,
                    out_specs=vmem,
                    compiler_params=params,
                    cost_estimate=cost(0),
                    name="modes",
                )(t_high, t_low, both)
            )
        early = early + late + [((chunk, 0), made[H - 1])]
        late = [((chunk, d), swap(made[H - 1 - d], "col", 2 * d)) for d in range(1, H)]
    return assemble(late, [assemble(early, [])])


def solution(mesh):
    return jax.shard_map(
        per_device,
        mesh=mesh,
        in_specs=(
            P("row", ("tm", "col")),
            P("row", ("tm", "col")),
            P("col", ("tm", "row")),
            P("col", ("tm", "row")),
            P(None, ("tm", "col")),
            P(None, ("tm", "col")),
            P("tm"),
            P(),
        ),
        out_specs=P("tm", "col", "row"),
        check_vma=False,
    )
```
